512 devices in a mesh: seq: 128 (over y, z, core), head: 4 (over x).
Axes of the slice: x: 4, y: 4, z: 16, core: 2. Of those that a mesh axis runs over, the one named last changes fastest.
Arguments:
- ids: int32 [256, 256], P('seq'), may hold values from 0 to 32
- pad_mask: int32 [256], P('seq'), may hold values from 0 to 1, as said below
- embed: bfloat16 [33, 768], replicated, may hold values from -16 to 16
- row_qkv: bfloat16 [3, 768, 768], P(None, 'head'), may hold values from -24 to 24
- row_out: bfloat16 [768, 768], P('head'), may hold values from -0.4375 to 0.4375
- col_qkv: bfloat16 [3, 768, 768], P(None, 'head'), may hold values from -24 to 24
- col_out: bfloat16 [768, 768], P('head'), may hold values from -0.21875 to 0.21875
Outputs:
- layer_out: bfloat16 [256, 256, 768], P('seq', None, 'head')
The draws below stay inside these ranges and needn't reach their ends.
Inputs may be any that keep to these rules, and one draw needn't show every extreme that they name: `pad_mask`: sequence 0 is always real.
All inputs are finite; a program needn't handle non-finite values.
Results may differ from the reference program's by a relative error of at most 0.007.
Values may be sent and summed in bfloat16 or wider, within the bound.
A program may use at most 64 MiB of HBM per device.

```python
import math
import jax
import jax.numpy as jnp
import numpy as np
from jax import lax

D = 768
HEADS = 12
HEAD_DIM = 64
VOCAB = 33
COLS = 256
ROWS = 256


def weight_block(key, query_gain):
    first = jax.random.fold_in(key, 0)
    base = jnp.clip(jax.random.normal(first, (3, D, D), jnp.float32), -4.0, 4.0) * D ** (-0.5)
    key_weight = base[1]
    return jnp.swapaxes(jnp.stack([query_gain * base[0], key_weight, base[2]]), 1, 2)


def draw_row_qkv(key, part):
    key = jax.random.fold_in(key, 21)
    block = weight_block(key, 2.0)
    return block.astype(jnp.bfloat16)


def draw_col_qkv(key, part):
    key = jax.random.fold_in(key, 22)
    block = weight_block(key, 1.0)
    return block.astype(jnp.bfloat16)


def draw_embed(key, part):
    key = jax.random.fold_in(key, 11)
    first, second, third = jax.random.split(key, 3)
    col_scale = jnp.exp(jax.random.uniform(second, (1, D), jnp.float32, 0.0, math.log(10.0)))
    row_scale = jnp.exp(jax.random.uniform(third, (VOCAB, 1), jnp.float32, 0.0, math.log(4.0)))
    base = jnp.clip(jax.random.normal(first, (VOCAB, D), jnp.float32), -4.0, 4.0)
    return (base * col_scale * row_scale * 0.1).astype(jnp.bfloat16)


def draw_pad_mask(key, part):
    key = jax.random.fold_in(key, 31)
    position = jnp.arange(ROWS, dtype=jnp.int32)
    ticket = jax.random.randint(key, (ROWS,), 0, 1000, jnp.int32)
    limit = 1000 - 800 * position // ROWS
    live = jnp.logical_or(ticket < limit, position == 0)
    return live.astype(jnp.int32)


def set_ends(entries, stream_key, least, largest):
    spot = [jax.random.randint(jax.random.fold_in(stream_key, axis), (), 0, length) for axis, length in enumerate(entries.shape)]
    widest = entries.shape.index(max(entries.shape))
    beside = spot[:widest] + [(spot[widest] + 1) % entries.shape[widest]] + spot[widest + 1:]
    return entries.at[tuple(spot)].set(least).at[tuple(beside)].set(largest)


def block_scale(own_key, extent, cuts, least, high):
    gain = 1.0
    for axis_at, shards_of in cuts:
        heights = jax.random.uniform(jax.random.fold_in(jax.random.fold_in(own_key, 6), axis_at), (shards_of,), jnp.float32, least / len(cuts), high / len(cuts))
        gain = gain * jnp.repeat(jnp.exp(heights), extent[axis_at] // shards_of).reshape((-1,) + (1,) * (len(extent) - 1 - axis_at))
    return gain


def rank_table(count, skew):
    weights = [(1 << 20) // math.isqrt(standing ** skew) + 1 for standing in range(1, count + 1)]
    scale = 1 + sum(weights) // (1 << 30)
    return np.cumsum(np.array([max(1, weight // scale) for weight in weights]))


def skewed_ids(own_key, dims, amount, slope):
    listing = rank_table(amount, slope)
    pick = jax.random.randint(jax.random.fold_in(own_key, 1), dims, 0, int(listing[amount - 1]))
    grade = jnp.searchsorted(jnp.asarray(listing, jnp.int32), pick, side="right")
    return jax.random.permutation(jax.random.fold_in(own_key, 2), amount)[grade].astype(jnp.int32)


def gaussian(stream_key, shape, deviation, reach, pieces=(), held_as=jnp.bfloat16):
    loudness = block_scale(stream_key, shape, pieces, -0.22, 0.18) if pieces else 1.0
    values = jax.random.normal(stream_key, shape, jnp.float32) * deviation * loudness
    return jnp.minimum(jnp.maximum(values, -reach), reach).astype(held_as)


def setup_inputs(seed: int = 0) -> dict:
    seeds = jax.random.split(jax.random.key(seed), 8)
    ids = set_ends(skewed_ids(seeds[0], (ROWS, COLS), VOCAB, 1), jax.random.fold_in(seeds[0], 3), 0, VOCAB - 1).astype(jnp.int32)
    pad_mask = draw_pad_mask(jax.random.fold_in(seeds[7], 71), 0)
    embed = draw_embed(jax.random.fold_in(seeds[7], 71), 0)
    row_qkv = draw_row_qkv(jax.random.fold_in(seeds[7], 71), 0)
    row_out = gaussian(seeds[4], (D, D), (D // 4) ** -0.5, 0.4375, ((0, 4),))
    col_qkv = draw_col_qkv(jax.random.fold_in(seeds[7], 71), 0)
    col_out = gaussian(seeds[6], (D, D), D ** -0.5, 0.21875, ((0, 4),))
    return {"ids": ids, "pad_mask": pad_mask, "embed": embed, "row_qkv": row_qkv, "row_out": row_out, "col_qkv": col_qkv, "col_out": col_out}


EPS = 1e-05

def layer_norm(values):
    mean = lax.optimization_barrier(jnp.mean(values, axis=-1, keepdims=True))
    centred = values - mean
    spread = lax.optimization_barrier(jnp.mean(centred * centred, axis=-1, keepdims=True))
    return centred * lax.rsqrt(spread + EPS)

def softmax_last(scores):
    top = lax.optimization_barrier(jnp.max(scores, axis=-1, keepdims=True))
    weights = jnp.exp(scores - top)
    return weights / lax.optimization_barrier(jnp.sum(weights, axis=-1, keepdims=True))

def project(inputs, weights):
    product = jnp.einsum('rcd,ted->trce', inputs.astype(jnp.float32), weights.astype(jnp.float32))
    return product.astype(jnp.bfloat16)

def reference(ids, pad_mask, embed, row_qkv, row_out, col_qkv, col_out):
    embedded = embed.astype(jnp.float32)[ids]
    normed = layer_norm(embedded).astype(jnp.bfloat16)
    row_proj = project(normed, row_qkv)
    live = pad_mask.astype(jnp.float32)
    count = jnp.sum(live)
    head_shape = (ROWS, COLS, HEADS, HEAD_DIM)
    query = (row_proj[0].astype(jnp.float32) * live[:, None, None]).reshape(head_shape)
    keys = row_proj[1].astype(jnp.float32).reshape(head_shape)
    values = row_proj[2].astype(jnp.float32).reshape(head_shape)
    tied = jnp.einsum('rihd,rjhd->hij', query, keys) * (HEAD_DIM ** (-0.5) / jnp.sqrt(count))
    row_probs = softmax_last(tied).astype(jnp.bfloat16)
    row_context = jnp.einsum('hij,rjhd->rihd', row_probs.astype(jnp.float32), values)
    row_context = row_context.astype(jnp.bfloat16).reshape(ROWS, COLS, D)
    mixed = embedded + jnp.einsum('rce,fe->rcf', row_context.astype(jnp.float32), row_out.astype(jnp.float32))
    normed_second = layer_norm(mixed).astype(jnp.bfloat16)
    col_proj = project(normed_second, col_qkv)
    by_column = jnp.moveaxis(col_proj, 2, 0)

    def one_column(block):
        shape = (ROWS, HEADS, HEAD_DIM)
        col_query = block[0].astype(jnp.float32).reshape(shape)
        col_keys = block[1].astype(jnp.float32).reshape(shape)
        col_values = block[2].astype(jnp.float32).reshape(shape)
        scores = jnp.einsum('rhd,shd->hrs', col_query, col_keys) * HEAD_DIM ** (-0.5)
        scores = jnp.where(live > 0, scores, -jnp.inf)
        probs = softmax_last(scores).astype(jnp.bfloat16)
        context = jnp.einsum('hrs,shd->rhd', probs.astype(jnp.float32), col_values)
        return context.astype(jnp.bfloat16).reshape(ROWS, D)
    col_context = jnp.moveaxis(lax.map(one_column, by_column), 0, 1)
    layer_out = mixed + jnp.einsum('rce,fe->rcf', col_context.astype(jnp.float32), col_out.astype(jnp.float32))
    return layer_out.astype(jnp.bfloat16)
```

```python
import jax
import jax.numpy as jnp
from jax import lax
from jax.experimental import pallas as pl
from jax.experimental.pallas import tpu as pltpu
from jax.sharding import PartitionSpec as P

HEAD_DIM = 64
EPS = 1e-05
NX, NY, NZ, NC = 4, 4, 16, 2
VOCAB = 33
D = 768
DH = 192
COLS = 256
ROWS = 256
HP = 16
VH = VOCAB * HP
MESH = pl.DeviceIdType.MESH
F32 = jnp.float32
BF16 = jnp.bfloat16


def dot(a, b, ca=1, cb=0):
    return lax.dot_general(a, b, (((ca,), (cb,)), ((), ())), preferred_element_type=F32)


def norm_rows(values):
    mean = jnp.mean(values, axis=1, keepdims=True)
    centred = values - mean
    spread = jnp.mean(centred * centred, axis=1, keepdims=True)
    return centred * lax.rsqrt(spread + EPS)


def norm_cols(values):
    mean = jnp.mean(values, axis=0, keepdims=True)
    centred = values - mean
    spread = jnp.mean(centred * centred, axis=0, keepdims=True)
    return centred * lax.rsqrt(spread + EPS)


def iota(shape, dim):
    return lax.broadcasted_iota(jnp.int32, shape, dim)


def kernel(
    ids_ref, mask_ref, embed_ref, rqkv_ref, rout_ref, cqkv_ref, cout_ref,
    out_ref,
    idbuf, tab, wro, wco, emb_s, sel_s, qt_s, kf_s, vf_s, kx_s, vxt_s, oh_s, t_s, wm_s,
    mixed_s, ctxs, ctxr, sa, ra, sb,
    zs, zr, ys, yr, ts, tr, ros, ror, rfs, rfr, cos, cor, cfs, cfr, xs, xr, as_, ar, bs, br, ls,
):
    s = lax.axis_index("seq")
    x = lax.axis_index("head")
    y = lax.div(s, NZ * NC)
    z = lax.rem(lax.div(s, NC), NZ)
    core = lax.rem(s, NC)
    grp = y * NC + core
    half = lax.rem(x, 2)
    col_in = lax.div(x, 2)

    def seq_at(yy, zz, cc):
        return (yy * NZ + zz) * NC + cc

    barrier = pltpu.get_barrier_semaphore()

    def greet_line(k, carry):
        pl.semaphore_signal(barrier, inc=1, device_id=(seq_at(y, lax.rem(z + k, NZ), core), x), device_id_type=MESH)
        return carry

    def greet_plane(k, carry):
        place = lax.rem(x * 8 + grp + k, 32)
        px, pg = lax.div(place, 8), lax.rem(place, 8)
        pl.semaphore_signal(
            barrier, inc=1, device_id=(seq_at(lax.div(pg, NC), z, lax.rem(pg, NC)), px), device_id_type=MESH)
        return carry

    lax.fori_loop(1, NZ, greet_line, 0)
    lax.fori_loop(1, 32, greet_plane, 0)

    slot = grp * NZ + z
    m0 = mask_ref[0]
    m1 = mask_ref[1]
    idbuf[slot, :, 0:COLS] = ids_ref[0:1, :] + ids_ref[1:2, :] * 65536
    idbuf[slot, :, COLS:COLS + 128] = jnp.zeros((1, 128), jnp.int32) + (m0 + m1 * 65536)

    pl.semaphore_wait(barrier, NZ - 1 + 31)

    def z_copy(k):
        return pltpu.make_async_remote_copy(
            src_ref=idbuf.at[slot], dst_ref=idbuf.at[slot], send_sem=zs.at[k], recv_sem=zr.at[k],
            device_id=(seq_at(y, lax.rem(z + k, NZ), core), x), device_id_type=MESH)

    def z_arrival(k):
        from_slot = grp * NZ + lax.rem(z + NZ - k, NZ)
        return pltpu.make_async_remote_copy(
            src_ref=idbuf.at[from_slot], dst_ref=idbuf.at[from_slot], send_sem=zs.at[k], recv_sem=zr.at[k],
            device_id=(seq_at(y, lax.rem(z + k, NZ), core), x), device_id_type=MESH)

    def z_start(k, carry):
        z_copy(k).start()
        return carry

    lax.fori_loop(1, NZ, z_start, 0)

    part = pl.ds(pl.multiple_of(core * 96, 96), 96)

    def weight_copy(src, buf, ss, rs, k):
        return pltpu.make_async_remote_copy(
            src_ref=src.at[part, :], dst_ref=buf.at[x, part, :], send_sem=ss.at[k], recv_sem=rs.at[k],
            device_id=(s, lax.rem(x + k, NX)), device_id_type=MESH)

    def weight_arrival(src, buf, ss, rs, k):
        xf = lax.rem(x + NX - k, NX)
        return pltpu.make_async_remote_copy(
            src_ref=src.at[part, :], dst_ref=buf.at[xf, part, :], send_sem=ss.at[k], recv_sem=rs.at[k],
            device_id=(s, lax.rem(x + k, NX)), device_id_type=MESH)

    def forward_copy(buf, ss, rs, k):
        xf = lax.rem(x + NX - k, NX)
        return pltpu.make_async_remote_copy(
            src_ref=buf.at[xf, part, :], dst_ref=buf.at[xf, part, :], send_sem=ss.at[k], recv_sem=rs.at[k],
            device_id=(s + 1 - 2 * core, x), device_id_type=MESH)

    def forward_arrival(buf, ss, rs, k):
        xf = lax.rem(x + NX - k, NX)
        other = pl.ds(pl.multiple_of((1 - core) * 96, 96), 96)
        return pltpu.make_async_remote_copy(
            src_ref=buf.at[xf, other, :], dst_ref=buf.at[xf, other, :], send_sem=ss.at[k], recv_sem=rs.at[k],
            device_id=(s + 1 - 2 * core, x), device_id_type=MESH)

    for k in range(1, NX):
        weight_copy(rout_ref, wro, ros, ror, k).start()

    emb_s[...] = jnp.zeros_like(emb_s)
    emb_s[0:VOCAB, :] = embed_ref[...].astype(F32)
    normed = norm_rows(emb_s[...]).astype(BF16)[0:48, :]
    tab[x] = jnp.zeros((144, 256), BF16)
    for t in range(3):
        tab[x, t * 48:(t + 1) * 48, 0:DH] = dot(normed, rqkv_ref[t], 1, 1).astype(BF16)

    def table_copy(k):
        return pltpu.make_async_remote_copy(
            src_ref=tab.at[x], dst_ref=tab.at[x], send_sem=ts.at[k], recv_sem=tr.at[k],
            device_id=(s, lax.rem(x + k, NX)), device_id_type=MESH)

    def table_arrival(k):
        xf = lax.rem(x + NX - k, NX)
        return pltpu.make_async_remote_copy(
            src_ref=tab.at[xf], dst_ref=tab.at[xf], send_sem=ts.at[k], recv_sem=tr.at[k],
            device_id=(s, lax.rem(x + k, NX)), device_id_type=MESH)

    for k in range(1, NX):
        table_copy(k).start()
    for k in range(1, NX):
        weight_copy(cout_ref, wco, cos, cor, k).start()
    wro[x] = rout_ref[...]
    wco[x] = cout_ref[...]

    emb_t = emb_s[...].T.astype(BF16)
    spot = iota((4 * 256, D), 0)
    goal = lax.div(spot, 256) * DH + lax.rem(spot, 256)
    sel_s[...] = jnp.where(
        jnp.logical_and(goal == iota((4 * 256, D), 1), lax.rem(spot, 256) < DH), 1.0, 0.0).astype(BF16)

    def z_wait(k, carry):
        z_arrival(k).wait_recv()
        return carry

    lax.fori_loop(1, NZ, z_wait, 0)

    def y_copy(k):
        to = lax.rem(grp + k, 8)
        mine = pl.ds(grp * NZ, NZ)
        return pltpu.make_async_remote_copy(
            src_ref=idbuf.at[mine], dst_ref=idbuf.at[mine], send_sem=ys.at[k], recv_sem=yr.at[k],
            device_id=(seq_at(lax.div(to, NC), z, lax.rem(to, NC)), x), device_id_type=MESH)

    def y_arrival(k):
        to = lax.rem(grp + k, 8)
        theirs = pl.ds(lax.rem(grp + 8 - k, 8) * NZ, NZ)
        return pltpu.make_async_remote_copy(
            src_ref=idbuf.at[theirs], dst_ref=idbuf.at[theirs], send_sem=ys.at[k], recv_sem=yr.at[k],
            device_id=(seq_at(lax.div(to, NC), z, lax.rem(to, NC)), x), device_id_type=MESH)

    for k in range(1, 8):
        y_copy(k).start()

    for k in range(1, NX):
        table_arrival(k).wait_recv()
    gathered = jnp.concatenate([tab[i] for i in range(NX)], axis=1)
    tables = dot(gathered, sel_s[...])
    qt_s[...] = jnp.zeros_like(qt_s)
    qt_s[0:48, :] = tables[0:48].astype(BF16)
    kf_s[...] = tables[48:96]
    vf_s[...] = jnp.zeros_like(vf_s)
    vf_s[0:48, :] = tables[96:144]
    own_head = jnp.where(iota((HP, D), 0) == lax.div(iota((HP, D), 1), HEAD_DIM), 1.0, 0.0)

    def expand(b, carry):
        kx_s[pl.ds(pl.multiple_of(b * HP, HP), HP), :] = (kf_s[pl.ds(b, 1), :] * own_head).astype(BF16)
        return carry

    lax.fori_loop(0, VOCAB, expand, 0)
    rep = jnp.where(iota((128, 640), 0) == lax.div(iota((128, 640), 1), HP), 1.0, 0.0).astype(BF16)
    head_of = jnp.where(
        lax.div(iota((D, 640), 0), HEAD_DIM) == lax.rem(iota((D, 640), 1), HP), 1.0, 0.0)
    vxt_s[...] = (dot(vf_s[...].T.astype(BF16), rep) * head_of).astype(BF16)

    for k in range(1, NX):
        weight_arrival(rout_ref, wro, ros, ror, k).wait_recv()
        forward_copy(wro, rfs, rfr, k).start()

    for k in range(1, 8):
        y_arrival(k).wait_recv()

    words = idbuf[:, 0, :]
    low = lax.bitwise_and(words, 65535).astype(F32)
    high = lax.shift_right_logical(words, 16).astype(F32)
    table = jnp.concatenate([low[0:64], high[0:64], low[64:128], high[64:128]], axis=0)
    ids = table[:, 0:COLS].astype(BF16)
    live = table[:, COLS:COLS + 128]
    live2 = jnp.concatenate([live, live], axis=1)
    count = jnp.sum(live2, axis=0, keepdims=True)
    wm_s[0, 0:ROWS, :] = ids

    def onehots(b, carry):
        held = wm_s[0, 0:ROWS, :].astype(F32)
        oh_s[pl.ds(pl.multiple_of(b * ROWS, ROWS), ROWS), :] = jnp.where(
            held == b.astype(F32), 1.0, 0.0).astype(BF16)
        return carry

    lax.fori_loop(0, VOCAB, onehots, 0)

    first_col = z * 16 + grp * 2
    own = []
    for i in range(2):
        pick = jnp.where(iota((128, COLS), 1) == first_col + i, 1.0, 0.0).astype(BF16)
        as_row = dot(pick, ids, 1, 1)
        own.append(jnp.where(as_row == iota((128, ROWS), 0).astype(F32), 1.0, 0.0).astype(BF16))
        pick_t = jnp.where(iota((COLS, 128), 0) == first_col + i, 1.0, 0.0).astype(BF16)
        as_col = dot(ids, pick_t)
        own_t = (jnp.where(as_col == iota((ROWS, 128), 1).astype(F32), 1.0, 0.0) * live).astype(BF16)
        query = dot(own_t, qt_s[...]).astype(BF16)
        score = dot(kx_s[...], query, 1, 1)
        upper = score.astype(BF16)
        lower = (score - upper.astype(F32)).astype(BF16)
        for b in range(VOCAB):
            t_s[i * 32:i * 32 + 16, b * ROWS:(b + 1) * ROWS] = upper[b * HP:(b + 1) * HP]
            t_s[i * 32 + 16:i * 32 + 32, b * ROWS:(b + 1) * ROWS] = lower[b * HP:(b + 1) * HP]

    tied4 = dot(t_s[...], oh_s[...])
    tied = jnp.concatenate([tied4[0:16] + tied4[16:32], tied4[32:48] + tied4[48:64]], axis=0)
    tied = tied * (HEAD_DIM ** (-0.5) * lax.rsqrt(count))
    top = jnp.max(tied, axis=1, keepdims=True)
    weights = jnp.exp(tied - top)
    probs = (weights / jnp.sum(weights, axis=1, keepdims=True)).astype(BF16)

    for b in range(VOCAB):
        share = dot(probs, oh_s[b * ROWS:(b + 1) * ROWS, :], 1, 1)
        wm_s[0, b * HP:(b + 1) * HP, :] = share[0:16].astype(BF16)
        wm_s[1, b * HP:(b + 1) * HP, :] = share[16:32].astype(BF16)

    for k in range(1, NX):
        forward_arrival(wro, rfs, rfr, k).wait_recv()
    row_weight = wro[...].reshape(D, D)
    col_weight = cqkv_ref[...].reshape(3 * DH, D)
    live_here = live2 > 0.0

    def x_copy(to):
        return pltpu.make_async_remote_copy(
            src_ref=ctxs.at[to], dst_ref=ctxr.at[x], send_sem=xs.at[to], recv_sem=xr.at[x],
            device_id=(s, to), device_id_type=MESH)

    def x_arrival(xf):
        return pltpu.make_async_remote_copy(
            src_ref=ctxs.at[xf], dst_ref=ctxr.at[xf], send_sem=xs.at[xf], recv_sem=xr.at[xf],
            device_id=(s, xf), device_id_type=MESH)

    for i in range(2):
        context = dot(vxt_s[:, 0:VH], wm_s[i]).astype(BF16)
        mixed = dot(row_weight, context) + dot(emb_t, own[i])
        mixed_s[2 * i] = mixed[:, 0:128]
        mixed_s[2 * i + 1] = mixed[:, 128:256]
        normed2 = norm_cols(mixed).astype(BF16)
        proj = dot(col_weight, normed2)
        queries = (proj[0:DH].astype(BF16) * jnp.asarray(0.125, BF16))
        keys = jnp.concatenate([proj[DH:2 * DH], jnp.zeros((64, ROWS), F32)], axis=0).T.astype(BF16)
        values = proj[2 * DH:3 * DH].astype(BF16)
        for h in range(3):
            pieces = []
            if h > 0:
                pieces.append(jnp.zeros((64 * h, ROWS), BF16))
            pieces.append(queries[64 * h:64 * h + 64])
            pieces.append(jnp.zeros((256 - 64 * h - 64, ROWS), BF16))
            scores = dot(keys, jnp.concatenate(pieces, axis=0))
            scores = jnp.where(live_here, scores, -1e38)
            raw = jnp.exp(scores - jnp.max(scores, axis=0, keepdims=True))
            total = jnp.sum(raw, axis=0, keepdims=True)
            got = (dot(values[64 * h:64 * h + 64], raw.astype(BF16)) / total).astype(BF16)
            ctxs[2 * i, 64 * h:64 * h + 64, :] = got[:, 0:128]
            ctxs[2 * i + 1, 64 * h:64 * h + 64, :] = got[:, 128:256]
        for to in (2 * i, 2 * i + 1):
            @pl.when(x != to)
            def _():
                x_copy(to).start()

            @pl.when(x == to)
            def _():
                ctxr[to] = ctxs[to]

    for k in range(1, NX):
        weight_arrival(cout_ref, wco, cos, cor, k).wait_recv()
        forward_copy(wco, cfs, cfr, k).start()
    for k in range(1, NX):
        forward_arrival(wco, cfs, cfr, k).wait_recv()
    for xf in range(NX):
        @pl.when(x != xf)
        def _():
            x_arrival(xf).wait_recv()

    done = dot(wco[...].reshape(D, D), ctxr[...].reshape(D, 128)) + mixed_s[x]

    def a_copy(to_x, g):
        to_y = 2 * half + g // 2
        return pltpu.make_async_remote_copy(
            src_ref=sa.at[to_x, g], dst_ref=ra.at[grp * 2 + col_in],
            send_sem=as_.at[to_x * 4 + g], recv_sem=ar.at[grp * 2 + col_in],
            device_id=(seq_at(to_y, z, g % 2), to_x), device_id_type=MESH)

    def a_self(to_x, g):
        return jnp.logical_and(x == to_x, jnp.logical_and(y == 2 * half + g // 2, core == g % 2))

    for to_x in range(NX):
        turned = done[DH * to_x:DH * (to_x + 1)].T
        wide = jnp.concatenate([turned[0:64], turned[64:128]], axis=1).astype(BF16)
        for g in range(4):
            sa[to_x, g] = wide[16 * g:16 * g + 16]
        for g in range(4):
            @pl.when(jnp.logical_not(a_self(to_x, g)))
            def _():
                a_copy(to_x, g).start()

            @pl.when(a_self(to_x, g))
            def _():
                ra[grp * 2 + col_in] = sa[to_x, g]

    def a_from_self(k):
        return jnp.logical_and(grp == k // 2, x == 2 * (k % 2) + lax.div(y, 2))

    def a_arrival(k):
        from_x = 2 * (k % 2) + lax.div(y, 2)
        g = k // 2
        return pltpu.make_async_remote_copy(
            src_ref=ra.at[k], dst_ref=ra.at[k], send_sem=as_.at[k], recv_sem=ar.at[k],
            device_id=(seq_at(g // 2, z, g % 2), from_x), device_id_type=MESH)

    for k in range(16):
        @pl.when(jnp.logical_not(a_from_self(k)))
        def _():
            a_arrival(k).wait_recv()

    order = iota((256, 256), 0)
    swap = jnp.where(lax.rem(order, 16) * 16 + lax.div(order, 16) == iota((256, 256), 1), 1.0, 0.0).astype(BF16)
    sb[...] = dot(swap, ra[...].reshape(256, 384)).astype(BF16)
    place = pl.ds(pl.multiple_of(z * 16, 16), 16)

    def b_copy(k):
        to_z = lax.rem(z + k, NZ)
        return pltpu.make_async_remote_copy(
            src_ref=sb.at[pl.ds(pl.multiple_of(to_z * 16, 16), 16), :], dst_ref=out_ref.at[place, :],
            send_sem=bs.at[k], recv_sem=br.at[k],
            device_id=(seq_at(y, to_z, core), x), device_id_type=MESH)

    def b_arrival(k):
        from_z = lax.rem(z + NZ - k, NZ)
        spot_z = pl.ds(pl.multiple_of(from_z * 16, 16), 16)
        return pltpu.make_async_remote_copy(
            src_ref=sb.at[spot_z, :], dst_ref=out_ref.at[spot_z, :],
            send_sem=bs.at[k], recv_sem=br.at[k],
            device_id=(seq_at(y, lax.rem(z + k, NZ), core), x), device_id_type=MESH)

    def b_start(k, carry):
        b_copy(k).start()
        return carry

    lax.fori_loop(1, NZ, b_start, 0)
    keep = pltpu.make_async_copy(sb.at[place, :], out_ref.at[place, :], ls.at[0])
    keep.start()

    def z_done(k, carry):
        z_copy(k).wait_send()
        return carry

    lax.fori_loop(1, NZ, z_done, 0)
    for k in range(1, 8):
        y_copy(k).wait_send()
    for k in range(1, NX):
        table_copy(k).wait_send()
        weight_copy(rout_ref, wro, ros, ror, k).wait_send()
        weight_copy(cout_ref, wco, cos, cor, k).wait_send()
        forward_copy(wro, rfs, rfr, k).wait_send()
        forward_copy(wco, cfs, cfr, k).wait_send()
    for to in range(NX):
        @pl.when(x != to)
        def _():
            x_copy(to).wait_send()
    for to_x in range(NX):
        for g in range(4):
            @pl.when(jnp.logical_not(a_self(to_x, g)))
            def _():
                a_copy(to_x, g).wait_send()
    keep.wait()

    def b_done(k, carry):
        b_copy(k).wait_send()
        b_arrival(k).wait_recv()
        return carry

    lax.fori_loop(1, NZ, b_done, 0)


def body(ids, pad_mask, embed, row_qkv, row_out, col_qkv, col_out):
    vmem = pl.BlockSpec(memory_space=pltpu.VMEM)
    smem = pl.BlockSpec(memory_space=pltpu.SMEM)
    dma = pltpu.SemaphoreType.DMA
    got = pl.pallas_call(
        kernel,
        out_shape=jax.ShapeDtypeStruct((COLS, 2 * DH), BF16),
        in_specs=[vmem, smem, vmem, vmem, vmem, vmem, vmem],
        out_specs=pl.BlockSpec(memory_space=pl.ANY),
        scratch_shapes=[
            pltpu.VMEM((128, 1, 384), jnp.int32),
            pltpu.VMEM((NX, 144, 256), BF16),
            pltpu.VMEM((NX, DH, D), BF16),
            pltpu.VMEM((NX, DH, D), BF16),
            pltpu.VMEM((128, D), F32),
            pltpu.VMEM((1024, D), BF16),
            pltpu.VMEM((128, D), BF16),
            pltpu.VMEM((48, D), F32),
            pltpu.VMEM((128, D), F32),
            pltpu.VMEM((VH, D), BF16),
            pltpu.VMEM((D, 640), BF16),
            pltpu.VMEM((VOCAB * ROWS, COLS), BF16),
            pltpu.VMEM((64, VOCAB * ROWS), BF16),
            pltpu.VMEM((2, VH, ROWS), BF16),
            pltpu.VMEM((4, D, 128), F32),
            pltpu.VMEM((NX, DH, 128), BF16),
            pltpu.VMEM((NX, DH, 128), BF16),
            pltpu.VMEM((NX, 4, 16, 384), BF16),
            pltpu.VMEM((16, 16, 384), BF16),
            pltpu.VMEM((256, 384), BF16),
            dma((16,)), dma((16,)),
            dma((8,)), dma((8,)),
            dma((4,)), dma((4,)),
            dma((4,)), dma((4,)), dma((4,)), dma((4,)),
            dma((4,)), dma((4,)), dma((4,)), dma((4,)),
            dma((4,)), dma((4,)),
            dma((16,)), dma((16,)),
            dma((16,)), dma((16,)),
            dma((1,)),
        ],
        compiler_params=pltpu.CompilerParams(
            collective_id=0, has_side_effects=True, vmem_limit_bytes=48 * 1024 * 1024),
        cost_estimate=pl.CostEstimate(flops=6_000_000_000, bytes_accessed=4_000_000, transcendentals=500_000),
        name="msa_layer",
    )(ids, pad_mask, embed, row_qkv, row_out, col_qkv, col_out)
    return jnp.transpose(got.reshape(COLS, 2, DH), (1, 0, 2))


def solution(mesh):
    placed = (
        P("seq", None),
        P("seq"),
        P(),
        P(None, "head", None),
        P("head", None),
        P(None, "head", None),
        P("head", None),
    )
    return jax.shard_map(
        body, mesh=mesh, in_specs=placed, out_specs=P("seq", None, "head"), check_vma=False
    )
```

```python
import jax
import jax.numpy as jnp
from jax import lax
from jax.experimental import pallas as pl
from jax.experimental.pallas import tpu as pltpu
from jax.sharding import PartitionSpec as P

HEAD_DIM = 64
EPS = 1e-05
NX, NY, NZ, NC = 4, 4, 16, 2
VOCAB = 33
D = 768
DH = 192
COLS = 256
ROWS = 256
HP = 16
VH = VOCAB * HP
FAR_Z = (8, 9, 7, 10, 6, 11, 5, 12, 4, 13, 3, 14, 2, 15, 1)
FAR_Y = (4, 5, 3, 2, 6, 7, 1)
FAR_X = (2, 1, 3)
FAR_PLANE = (10, 11, 8, 9, 6, 7, 14, 15, 4, 5, 12, 13, 2, 3, 1, 0)
MESH = pl.DeviceIdType.MESH
F32 = jnp.float32
BF16 = jnp.bfloat16


def dot(a, b, ca=1, cb=0):
    return lax.dot_general(a, b, (((ca,), (cb,)), ((), ())), preferred_element_type=F32)


def norm_rows(values):
    mean = jnp.mean(values, axis=1, keepdims=True)
    centred = values - mean
    spread = jnp.mean(centred * centred, axis=1, keepdims=True)
    return centred * lax.rsqrt(spread + EPS)


def norm_cols(values):
    mean = jnp.mean(values, axis=0, keepdims=True)
    centred = values - mean
    spread = jnp.mean(centred * centred, axis=0, keepdims=True)
    return centred * lax.rsqrt(spread + EPS)


def iota(shape, dim):
    return lax.broadcasted_iota(jnp.int32, shape, dim)


class Exchange:
    opened = []

    def __init__(self, out, into, keys, sends=None, arrives=None):
        self.out, self.into, self.keys = out, into, keys
        self.sends = sends or (lambda k: None)
        self.arrives = arrives or (lambda k: None)
        Exchange.opened.append(self)
        self.waited = False

    def each(self, run, keys=None):
        for k in self.keys if keys is None else keys:
            run(k)

    def start(self, keys=None):
        def run(k):
            gate(self.sends(k), lambda: self.out(k).start())
        self.each(run, keys)

    def receive(self, keys=None):
        self.waited = True

        def run(k):
            gate(self.arrives(k), lambda: self.into(k).wait_recv())
        self.each(run, keys)

    def finish(self):
        def run(k):
            gate(self.sends(k), lambda: self.out(k).wait_send())
        self.each(run)


def gate(condition, action):
    if condition is None:
        action()
    else:
        pl.when(condition)(action)


def kernel(
    ids_hbm, mask_hbm, embed_hbm, rqkv_hbm, rout_hbm, cqkv_hbm, cout_hbm,
    out_ref,
    ids_ref, mask_ref, embed_ref, rqkv_ref, cqkv_ref,
    idbuf, tab, wro, wco, emb_s, sel_s, qt_s, kf_s, vf_s, kx_s, vxt_s, wm_s, sc_s,
    mixed_s, ctxs, ctxr, sa, ra, sb,
    zs, zr, ys, yr, ts, tr, ros, ror, rfs, rfr, cos, cor, cfs, cfr, xs, xr, as_, ar, bs, br, ls,
):
    Exchange.opened = []
    s = lax.axis_index("seq")
    x = lax.axis_index("head")
    y = lax.div(s, NZ * NC)
    z = lax.rem(lax.div(s, NC), NZ)
    core = lax.rem(s, NC)
    grp = y * NC + core
    half = lax.rem(x, 2)
    col_in = lax.div(x, 2)

    def seq_at(yy, zz, cc):
        return (yy * NZ + zz) * NC + cc

    def remote(src, dst, ss, rs, to_s, to_x):
        return pltpu.make_async_remote_copy(
            src_ref=src, dst_ref=dst, send_sem=ss, recv_sem=rs, device_id=(to_s, to_x), device_id_type=MESH)

    barrier = pltpu.get_barrier_semaphore()

    def greet_line(k, carry):
        pl.semaphore_signal(barrier, inc=1, device_id=(seq_at(y, lax.rem(z + k, NZ), core), x), device_id_type=MESH)
        return carry

    def greet_plane(k, carry):
        place = lax.rem(x * 8 + grp + k, 32)
        px, pg = lax.div(place, 8), lax.rem(place, 8)
        pl.semaphore_signal(
            barrier, inc=1, device_id=(seq_at(lax.div(pg, NC), z, lax.rem(pg, NC)), px), device_id_type=MESH)
        return carry

    lax.fori_loop(1, NZ, greet_line, 0)
    lax.fori_loop(1, 32, greet_plane, 0)
    fetch = [
        pltpu.make_async_copy(a, b, ls.at[i]) for i, (a, b) in enumerate((
            (ids_hbm, ids_ref), (mask_hbm, mask_ref), (embed_hbm, embed_ref), (rqkv_hbm, rqkv_ref),
            (rout_hbm, wro.at[x]), (cqkv_hbm, cqkv_ref), (cout_hbm, wco.at[x])))
    ]
    for copy in fetch:
        copy.start()

    slot = grp * NZ + z
    fetch[0].wait()
    fetch[1].wait()
    m0 = mask_ref[0]
    m1 = mask_ref[1]
    idbuf[slot, :, 0:COLS] = ids_ref[0:1, :] + ids_ref[1:2, :] * 65536
    idbuf[slot, :, COLS:COLS + 128] = jnp.zeros((1, 128), jnp.int32) + (m0 + m1 * 65536)

    fetch[2].wait()
    emb_s[...] = jnp.zeros_like(emb_s)
    emb_s[0:VOCAB, :] = embed_ref[...].astype(F32)
    normed = norm_rows(emb_s[...]).astype(BF16)[0:48, :]
    tab[x] = jnp.zeros((144, 256), BF16)
    fetch[3].wait()
    for t in range(3):
        tab[x, t * 48:(t + 1) * 48, 0:DH] = dot(normed, rqkv_ref[t], 1, 1).astype(BF16)

    pl.semaphore_wait(barrier, NZ - 1 + 31)

    def z_slot(k):
        return idbuf.at[grp * NZ + lax.rem(z + NZ - k, NZ)]

    ids_z = Exchange(
        lambda k: remote(idbuf.at[slot], idbuf.at[slot], zs.at[k], zr.at[k], seq_at(y, lax.rem(z + k, NZ), core), x),
        lambda k: remote(z_slot(k), z_slot(k), zs.at[k], zr.at[k], seq_at(y, lax.rem(z + k, NZ), core), x),
        FAR_Z)
    ids_z.start()

    part = pl.ds(pl.multiple_of(core * 96, 96), 96)
    other = pl.ds(pl.multiple_of((1 - core) * 96, 96), 96)
    ahead = lambda k: lax.rem(x + k, NX)
    behind = lambda k: lax.rem(x + NX - k, NX)

    def weight(src, buf, ss, rs):
        return Exchange(
            lambda k: remote(src.at[part, :], buf.at[x, part, :], ss.at[k], rs.at[k], s, ahead(k)),
            lambda k: remote(src.at[part, :], buf.at[behind(k), part, :], ss.at[k], rs.at[k], s, ahead(k)),
            FAR_X)

    def forward(buf, ss, rs):
        twin = s + 1 - 2 * core
        return Exchange(
            lambda k: remote(
                buf.at[behind(k), part, :], buf.at[behind(k), part, :], ss.at[k], rs.at[k], twin, x),
            lambda k: remote(
                buf.at[behind(k), other, :], buf.at[behind(k), other, :], ss.at[k], rs.at[k], twin, x),
            FAR_X)

    tabs = Exchange(
        lambda k: remote(tab.at[x], tab.at[x], ts.at[k], tr.at[k], s, ahead(k)),
        lambda k: remote(tab.at[behind(k)], tab.at[behind(k)], ts.at[k], tr.at[k], s, ahead(k)),
        FAR_X)
    tabs.start()
    row_out = weight(rout_hbm, wro, ros, ror)
    row_out.start()
    col_out = weight(cout_hbm, wco, cos, cor)

    emb_t = emb_s[...].T.astype(BF16)
    spot = iota((4 * 256, D), 0)
    goal = lax.div(spot, 256) * DH + lax.rem(spot, 256)
    sel_s[...] = jnp.where(
        jnp.logical_and(goal == iota((4 * 256, D), 1), lax.rem(spot, 256) < DH), 1.0, 0.0).astype(BF16)

    ids_z.receive()
    mine = pl.ds(grp * NZ, NZ)

    def y_seq(k):
        to = lax.rem(grp + k, 8)
        return seq_at(lax.div(to, NC), z, lax.rem(to, NC))

    def y_part(k):
        return idbuf.at[pl.ds(lax.rem(grp + 8 - k, 8) * NZ, NZ)]

    ids_y = Exchange(
        lambda k: remote(idbuf.at[mine], idbuf.at[mine], ys.at[k], yr.at[k], y_seq(k), x),
        lambda k: remote(y_part(k), y_part(k), ys.at[k], yr.at[k], y_seq(k), x),
        FAR_Y)
    ids_y.start()
    col_out.start()

    tabs.receive()
    gathered = jnp.concatenate([tab[i] for i in range(NX)], axis=1)
    tables = dot(gathered, sel_s[...])
    qt_s[...] = jnp.zeros_like(qt_s)
    qt_s[0:48, :] = tables[0:48].astype(BF16)
    kf_s[...] = tables[48:96]
    vf_s[...] = jnp.zeros_like(vf_s)
    vf_s[0:48, :] = tables[96:144]
    own_head = jnp.where(iota((HP, D), 0) == lax.div(iota((HP, D), 1), HEAD_DIM), 1.0, 0.0)

    def expand(b, carry):
        kx_s[pl.ds(pl.multiple_of(b * HP, HP), HP), :] = (kf_s[pl.ds(b, 1), :] * own_head).astype(BF16)
        return carry

    lax.fori_loop(0, VOCAB, expand, 0)
    scores_of = dot(kx_s[...], qt_s[...], 1, 1)
    upper = scores_of.astype(BF16)
    sc_s[0:VH, :] = upper
    sc_s[VH:2 * VH, :] = (scores_of - upper.astype(F32)).astype(BF16)
    rep = jnp.where(iota((128, 640), 0) == lax.div(iota((128, 640), 1), HP), 1.0, 0.0).astype(BF16)
    head_of = jnp.where(
        lax.div(iota((D, 640), 0), HEAD_DIM) == lax.rem(iota((D, 640), 1), HP), 1.0, 0.0)
    vxt_s[...] = (dot(vf_s[...].T.astype(BF16), rep) * head_of).astype(BF16)

    ids_y.receive()
    row_share = forward(wro, rfs, rfr)
    row_out.receive()
    row_share.start()

    words = idbuf[:, 0, :]
    low = lax.bitwise_and(words, 65535).astype(F32)
    high = lax.shift_right_logical(words, 16).astype(F32)
    table = jnp.concatenate([low[0:64], high[0:64], low[64:128], high[64:128]], axis=0)
    ids = table[:, 0:COLS].astype(BF16)
    live = table[:, COLS:COLS + 128]
    live2 = jnp.concatenate([live, live], axis=1)
    eye = jnp.where(iota((COLS, COLS), 0) == iota((COLS, COLS), 1), 1.0, 0.0).astype(BF16)
    ids_t = dot(eye, ids, 1, 1).astype(BF16)

    def onehot(of, b):
        return jnp.where(of == jnp.asarray(b, BF16), jnp.asarray(1, BF16), jnp.asarray(0, BF16))

    count = jnp.sum(live2, axis=0, keepdims=True)
    first_col = z * 16 + grp * 2
    token = iota((128, ROWS), 0).astype(F32)
    first_lane = jnp.where(iota((128, 128), 1) == 0, 1.0, 0.0).astype(BF16)
    live_row = dot(first_lane, live.astype(BF16), 1, 1)
    own, own_live = [], []
    for i in range(2):
        pick = jnp.where(iota((128, COLS), 1) == first_col + i, 1.0, 0.0).astype(BF16)
        hit = jnp.where(dot(pick, ids, 1, 1) == token, 1.0, 0.0)
        own.append(hit.astype(BF16))
        own_live.append((hit * live_row).astype(BF16))
    own = jnp.concatenate(own, axis=1)
    picked = dot(sc_s[...], jnp.concatenate(own_live, axis=1)).astype(BF16)
    sums = [None] * 4
    for b in range(VOCAB):
        left = jnp.concatenate([
            picked[b * HP:(b + 1) * HP, 0:ROWS], picked[VH + b * HP:VH + (b + 1) * HP, 0:ROWS],
            picked[b * HP:(b + 1) * HP, ROWS:], picked[VH + b * HP:VH + (b + 1) * HP, ROWS:]], axis=0)
        term = dot(left, onehot(ids, b))
        sums[b % 4] = term if sums[b % 4] is None else sums[b % 4] + term
    tied4 = (sums[0] + sums[1]) + (sums[2] + sums[3])
    tied = jnp.concatenate([tied4[0:16] + tied4[16:32], tied4[32:48] + tied4[48:64]], axis=0)
    tied = tied * (HEAD_DIM ** (-0.5) * lax.rsqrt(count))
    top = jnp.max(tied, axis=1, keepdims=True)
    weights = jnp.exp(tied - top)
    probs = (weights / jnp.sum(weights, axis=1, keepdims=True)).astype(BF16)

    for b in range(VOCAB):
        share = dot(probs, onehot(ids_t, b))
        wm_s[b * HP:(b + 1) * HP, 0:ROWS] = share[0:16].astype(BF16)
        wm_s[b * HP:(b + 1) * HP, ROWS:2 * ROWS] = share[16:32].astype(BF16)

    fetch[4].wait()
    fetch[5].wait()
    row_share.receive()
    row_weight = wro[...].reshape(D, D)
    col_weight = cqkv_ref[...].reshape(3 * DH, D)
    live_here = live2 > 0.0

    context = dot(vxt_s[:, 0:VH], wm_s[...]).astype(BF16)
    mixed = dot(row_weight, context) + dot(emb_t, own)
    for q in range(4):
        mixed_s[q] = mixed[:, 128 * q:128 * q + 128]
    proj = dot(col_weight, norm_cols(mixed).astype(BF16))
    scores, values = [], []
    for i in range(2):
        at = slice(i * ROWS, (i + 1) * ROWS)
        query = proj[0:DH, at].astype(BF16) * jnp.asarray(0.125, BF16)
        key = proj[DH:2 * DH, at].astype(BF16)
        value = proj[2 * DH:3 * DH, at].astype(BF16)
        for h in range(0, DH, HEAD_DIM):
            scores.append(dot(key[h:h + HEAD_DIM], query[h:h + HEAD_DIM], 0, 0))
            values.append(value[h:h + HEAD_DIM])
    weighted, totals = [], []
    for score in scores:
        score = jnp.where(live_here, score, -1e38)
        raw = jnp.exp(score - jnp.max(score, axis=0, keepdims=True))
        totals.append(1.0 / jnp.sum(raw, axis=0, keepdims=True))
        weighted.append(raw.astype(BF16))
    for q in range(6):
        got = (dot(values[q], weighted[q]) * totals[q]).astype(BF16)
        at = slice((q % 3) * HEAD_DIM, (q % 3 + 1) * HEAD_DIM)
        ctxs[q // 3 * 2, at, :] = got[:, 0:128]
        ctxs[q // 3 * 2 + 1, at, :] = got[:, 128:256]
    to_slot = Exchange(
        lambda k: remote(ctxs.at[ahead(k)], ctxr.at[x], xs.at[k], xr.at[k], s, ahead(k)),
        lambda k: remote(ctxs.at[ahead(k)], ctxr.at[behind(k)], xs.at[k], xr.at[k], s, ahead(k)),
        FAR_X)
    to_slot.start()
    col_share = forward(wco, cfs, cfr)
    col_out.receive()
    col_share.start()
    ctxr[x] = ctxs[x]

    fetch[6].wait()
    col_share.receive()
    to_slot.receive()

    done = dot(wco[...].reshape(D, D), ctxr[...].reshape(D, 128)) + mixed_s[x]

    def a_place(j):
        to_x = lax.rem(x + j // 4, NX)
        to_half = lax.rem(y + (j // 2) % 2, 2)
        return to_x, to_half, lax.rem(core + j % 2, 2)

    def a_out(j):
        to_x, to_half, to_core = a_place(j)
        k = grp * 2 + col_in
        return remote(
            sa.at[to_x, to_half * 2 + to_core], ra.at[k], as_.at[j], ar.at[k],
            seq_at(2 * half + to_half, z, to_core), to_x)

    def a_into(j):
        from_y = lax.rem(y + j // 4, NY)
        from_core = lax.rem(core + j % 2, 2)
        from_col = lax.rem(col_in + (j // 2) % 2, 2)
        k = (from_y * NC + from_core) * 2 + from_col
        return remote(
            ra.at[k], ra.at[k], as_.at[j], ar.at[k], seq_at(from_y, z, from_core), 2 * from_col + lax.div(y, 2))

    stays = half == lax.div(y, 2)
    to_plane = Exchange(
        a_out, a_into, FAR_PLANE,
        lambda j: jnp.logical_not(stays) if j == 0 else None,
        lambda j: jnp.logical_not(stays) if j == 0 else None)
    for to_x in range(NX):
        turned = done[DH * to_x:DH * (to_x + 1)].T
        wide = jnp.concatenate([turned[0:64], turned[64:128]], axis=1).astype(BF16)
        for g in range(4):
            sa[to_x, g] = wide[16 * g:16 * g + 16]
    to_plane.start()

    @pl.when(stays)
    def _():
        ra[grp * 2 + col_in] = sa[x, lax.rem(y, 2) * 2 + core]

    order = iota((256, 256), 0)
    swap = jnp.where(lax.rem(order, 16) * 16 + lax.div(order, 16) == iota((256, 256), 1), 1.0, 0.0).astype(BF16)
    to_plane.receive()

    sb[...] = dot(swap, ra[...].reshape(256, 384)).astype(BF16)

    def z_rows(at):
        return pl.ds(pl.multiple_of(at * 16, 16), 16)

    to_rows = Exchange(
        lambda k: remote(
            sb.at[z_rows(lax.rem(z + k, NZ)), :], out_ref.at[z_rows(z), :], bs.at[k], br.at[k],
            seq_at(y, lax.rem(z + k, NZ), core), x),
        lambda k: remote(
            sb.at[z_rows(lax.rem(z + NZ - k, NZ)), :], out_ref.at[z_rows(lax.rem(z + NZ - k, NZ)), :],
            bs.at[k], br.at[k], seq_at(y, lax.rem(z + k, NZ), core), x),
        tuple(range(1, NZ)))
    to_rows.start()
    keep = pltpu.make_async_copy(sb.at[z_rows(z), :], out_ref.at[z_rows(z), :], ls.at[7])
    keep.start()

    ids_z.finish()
    ids_y.finish()
    tabs.finish()
    for weights_sent in (row_out, col_out, row_share, col_share):
        weights_sent.finish()
    to_slot.finish()
    to_plane.finish()
    keep.wait()
    to_rows.receive()
    to_rows.finish()


def body(ids, pad_mask, embed, row_qkv, row_out, col_qkv, col_out):
    dma = pltpu.SemaphoreType.DMA
    got = pl.pallas_call(
        kernel,
        out_shape=jax.ShapeDtypeStruct((COLS, 2 * DH), BF16),
        in_specs=[pl.BlockSpec(memory_space=pltpu.HBM)] * 7,
        out_specs=pl.BlockSpec(memory_space=pl.ANY),
        scratch_shapes=[
            pltpu.VMEM((2, COLS), jnp.int32),
            pltpu.SMEM((2,), jnp.int32),
            pltpu.VMEM((VOCAB, D), BF16),
            pltpu.VMEM((3, DH, D), BF16),
            pltpu.VMEM((3, DH, D), BF16),
            pltpu.VMEM((128, 1, 384), jnp.int32),
            pltpu.VMEM((NX, 144, 256), BF16),
            pltpu.VMEM((NX, DH, D), BF16),
            pltpu.VMEM((NX, DH, D), BF16),
            pltpu.VMEM((128, D), F32),
            pltpu.VMEM((1024, D), BF16),
            pltpu.VMEM((128, D), BF16),
            pltpu.VMEM((48, D), F32),
            pltpu.VMEM((128, D), F32),
            pltpu.VMEM((VH, D), BF16),
            pltpu.VMEM((D, 640), BF16),
            pltpu.VMEM((VH, 2 * ROWS), BF16),
            pltpu.VMEM((2 * VH, 128), BF16),
            pltpu.VMEM((4, D, 128), F32),
            pltpu.VMEM((NX, DH, 128), BF16),
            pltpu.VMEM((NX, DH, 128), BF16),
            pltpu.VMEM((NX, 4, 16, 384), BF16),
            pltpu.VMEM((16, 16, 384), BF16),
            pltpu.VMEM((256, 384), BF16),
            dma((16,)), dma((16,)),
            dma((8,)), dma((8,)),
            dma((4,)), dma((4,)),
            dma((4,)), dma((4,)), dma((4,)), dma((4,)),
            dma((4,)), dma((4,)), dma((4,)), dma((4,)),
            dma((4,)), dma((4,)),
            dma((16,)), dma((16,)),
            dma((16,)), dma((16,)),
            dma((8,)),
        ],
        compiler_params=pltpu.CompilerParams(
            collective_id=0, has_side_effects=True, vmem_limit_bytes=63 * 1024 * 1024),
        cost_estimate=pl.CostEstimate(flops=6_000_000_000, bytes_accessed=4_000_000, transcendentals=500_000),
        name="msa_layer",
    )(ids, pad_mask, embed, row_qkv, row_out, col_qkv, col_out)
    return jnp.transpose(got.reshape(COLS, 2, DH), (1, 0, 2))


def solution(mesh):
    placed = (
        P("seq", None),
        P("seq"),
        P(),
        P(None, "head", None),
        P("head", None),
        P(None, "head", None),
        P("head", None),
    )
    return jax.shard_map(
        body, mesh=mesh, in_specs=placed, out_specs=P("seq", None, "head"), check_vma=False
    )
```

```python
import jax
import jax.numpy as jnp
from jax import lax
from jax.experimental import pallas as pl
from jax.experimental.pallas import tpu as pltpu
from jax.sharding import PartitionSpec as P

HEAD_DIM = 64
EPS = 1e-05
NX, NY, NZ, NC = 4, 4, 16, 2
VOCAB = 33
D = 768
DH = 192
COLS = 256
ROWS = 256
HP = 16
VH = VOCAB * HP
FAR_Z = (8, 9, 7, 10, 6, 11, 5, 12, 4, 13, 3, 14, 2, 15, 1)
FAR_Y = (4, 5, 3, 2, 6, 7, 1)
NEAR_Z = (-4, 3, -3, 2, -2, 1, -1)
NCOL = 4
FAR_X = (2, 1, 3)
FAR_PLANE = (10, 11, 8, 9, 6, 7, 14, 15, 4, 5, 12, 13, 2, 3, 1, 0)
MESH = pl.DeviceIdType.MESH
F32 = jnp.float32
BF16 = jnp.bfloat16


def dot(a, b, ca=1, cb=0):
    return lax.dot_general(a, b, (((ca,), (cb,)), ((), ())), preferred_element_type=F32)


def norm_rows(values):
    mean = jnp.mean(values, axis=1, keepdims=True)
    centred = values - mean
    spread = jnp.mean(centred * centred, axis=1, keepdims=True)
    return centred * lax.rsqrt(spread + EPS)


def norm_cols(values):
    mean = jnp.mean(values, axis=0, keepdims=True)
    centred = values - mean
    spread = jnp.mean(centred * centred, axis=0, keepdims=True)
    return centred * lax.rsqrt(spread + EPS)


def iota(shape, dim):
    return lax.broadcasted_iota(jnp.int32, shape, dim)


class Exchange:
    opened = []

    def __init__(self, out, into, keys, sends=None, arrives=None):
        self.out, self.into, self.keys = out, into, keys
        self.sends = sends or (lambda k: None)
        self.arrives = arrives or (lambda k: None)
        Exchange.opened.append(self)
        self.waited = False

    def each(self, run, keys=None):
        for k in self.keys if keys is None else keys:
            run(k)

    def start(self, keys=None):
        def run(k):
            gate(self.sends(k), lambda: self.out(k).start())
        self.each(run, keys)

    def receive(self, keys=None):
        self.waited = True

        def run(k):
            gate(self.arrives(k), lambda: self.into(k).wait_recv())
        self.each(run, self.keys[::-1] if keys is None else keys)

    def finish(self):
        def run(k):
            gate(self.sends(k), lambda: self.out(k).wait_send())
        self.each(run)


def gate(condition, action):
    if condition is None:
        action()
    else:
        pl.when(condition)(action)


def kernel(
    ids_hbm, mask_hbm, embed_hbm, rqkv_hbm, rout_hbm, cqkv_hbm, cout_hbm,
    out_ref,
    ids_ref, mask_ref, embed_ref, rqkv_ref, cqkv_ref,
    idbuf, tab, wro, wco, emb_s, sel_s, qt_s, kf_s, vf_s, kx_s, vxt_s, wm_s, vo_s, sc_s,
    mixed_s, ctxs, ctxr, sa, ra, sb,
    zs, zr, ys, yr, ts, tr, ros, ror, rfs, rfr, cos, cor, cfs, cfr, xs, xr, as_, ar, bs, br, ls,
):
    Exchange.opened = []
    s = lax.axis_index("seq")
    x = lax.axis_index("head")
    y = lax.div(s, NZ * NC)
    z = lax.rem(lax.div(s, NC), NZ)
    core = lax.rem(s, NC)
    grp = y * NC + core
    half = lax.rem(x, 2)
    col_in = lax.div(x, 2)
    odd = lax.rem(z, 2)
    first_z = lax.rem(z + NZ - 4 + odd, NZ)

    def seq_at(yy, zz, cc):
        return (yy * NZ + zz) * NC + cc

    def remote(src, dst, ss, rs, to_s, to_x):
        return pltpu.make_async_remote_copy(
            src_ref=src, dst_ref=dst, send_sem=ss, recv_sem=rs, device_id=(to_s, to_x), device_id_type=MESH)

    barrier = pltpu.get_barrier_semaphore()

    def greet_line(k, carry):
        pl.semaphore_signal(barrier, inc=1, device_id=(seq_at(y, lax.rem(z + k, NZ), core), x), device_id_type=MESH)
        return carry

    def greet_plane(k, carry):
        place = lax.rem(x * 8 + grp + k, 32)
        px, pg = lax.div(place, 8), lax.rem(place, 8)
        pl.semaphore_signal(
            barrier, inc=1, device_id=(seq_at(lax.div(pg, NC), z, lax.rem(pg, NC)), px), device_id_type=MESH)
        return carry

    lax.fori_loop(1, NZ, greet_line, 0)
    lax.fori_loop(1, 32, greet_plane, 0)
    fetch = [
        pltpu.make_async_copy(a, b, ls.at[i]) for i, (a, b) in enumerate((
            (ids_hbm, ids_ref), (mask_hbm, mask_ref), (embed_hbm, embed_ref), (rqkv_hbm, rqkv_ref),
            (rout_hbm, wro.at[x]), (cqkv_hbm, cqkv_ref), (cout_hbm, wco.at[x])))
    ]
    for copy in fetch:
        copy.start()

    slot = grp * NZ + z
    fetch[0].wait()
    fetch[1].wait()
    m0 = mask_ref[0]
    m1 = mask_ref[1]
    idbuf[slot, :, 0:COLS] = ids_ref[0:1, :] + ids_ref[1:2, :] * 65536
    idbuf[slot, :, COLS:COLS + 128] = jnp.zeros((1, 128), jnp.int32) + (m0 + m1 * 65536)

    fetch[2].wait()
    emb_s[...] = jnp.zeros_like(emb_s)
    emb_s[0:VOCAB, :] = embed_ref[...].astype(F32)
    normed = norm_rows(emb_s[...]).astype(BF16)[0:48, :]
    tab[x] = jnp.zeros((144, 256), BF16)
    fetch[3].wait()
    for t in range(3):
        tab[x, t * 48:(t + 1) * 48, 0:DH] = dot(normed, rqkv_ref[t], 1, 1).astype(BF16)

    pl.semaphore_wait(barrier, NZ - 1 + 31)

    def z_slot(k):
        return idbuf.at[grp * NZ + lax.rem(z + NZ - k, NZ)]

    ids_z = Exchange(
        lambda k: remote(idbuf.at[slot], idbuf.at[slot], zs.at[k], zr.at[k], seq_at(y, lax.rem(z + k, NZ), core), x),
        lambda k: remote(z_slot(k), z_slot(k), zs.at[k], zr.at[k], seq_at(y, lax.rem(z + k, NZ), core), x),
        FAR_Z)
    ids_z.start()

    part = pl.ds(pl.multiple_of(core * 96, 96), 96)
    other = pl.ds(pl.multiple_of((1 - core) * 96, 96), 96)
    ahead = lambda k: lax.rem(x + k, NX)
    behind = lambda k: lax.rem(x + NX - k, NX)

    def weight(src, buf, ss, rs):
        return Exchange(
            lambda k: remote(src.at[part, :], buf.at[x, part, :], ss.at[k], rs.at[k], s, ahead(k)),
            lambda k: remote(src.at[part, :], buf.at[behind(k), part, :], ss.at[k], rs.at[k], s, ahead(k)),
            FAR_X)

    def forward(buf, ss, rs):
        twin = s + 1 - 2 * core
        return Exchange(
            lambda k: remote(
                buf.at[behind(k), part, :], buf.at[behind(k), part, :], ss.at[k], rs.at[k], twin, x),
            lambda k: remote(
                buf.at[behind(k), other, :], buf.at[behind(k), other, :], ss.at[k], rs.at[k], twin, x),
            FAR_X)

    tabs = Exchange(
        lambda k: remote(tab.at[x], tab.at[x], ts.at[k], tr.at[k], s, ahead(k)),
        lambda k: remote(tab.at[behind(k)], tab.at[behind(k)], ts.at[k], tr.at[k], s, ahead(k)),
        FAR_X)
    tabs.start()
    row_out = weight(rout_hbm, wro, ros, ror)
    row_out.start()
    col_out = weight(cout_hbm, wco, cos, cor)

    vo_s[:, :, 640:768] = emb_s[...].T.astype(BF16).reshape(NX, DH, 128)
    spot = iota((4 * 256, D), 0)
    goal = lax.div(spot, 256) * DH + lax.rem(spot, 256)
    sel_s[...] = jnp.where(
        jnp.logical_and(goal == iota((4 * 256, D), 1), lax.rem(spot, 256) < DH), 1.0, 0.0).astype(BF16)

    ids_z.receive()
    mine = pl.ds(grp * NZ, NZ)

    def y_seq(k):
        to = lax.rem(grp + k, 8)
        return seq_at(lax.div(to, NC), z, lax.rem(to, NC))

    def y_part(k):
        return idbuf.at[pl.ds(lax.rem(grp + 8 - k, 8) * NZ, NZ)]

    ids_y = Exchange(
        lambda k: remote(idbuf.at[mine], idbuf.at[mine], ys.at[k], yr.at[k], y_seq(k), x),
        lambda k: remote(y_part(k), y_part(k), ys.at[k], yr.at[k], y_seq(k), x),
        FAR_Y)
    ids_y.start()
    col_out.start()

    tabs.receive()
    gathered = jnp.concatenate([tab[i] for i in range(NX)], axis=1)
    tables = dot(gathered, sel_s[...])
    qt_s[...] = jnp.zeros_like(qt_s)
    qt_s[0:48, :] = tables[0:48].astype(BF16)
    kf_s[...] = tables[48:96]
    vf_s[...] = jnp.zeros_like(vf_s)
    vf_s[0:48, :] = tables[96:144]
    own_head = jnp.where(iota((HP, D), 0) == lax.div(iota((HP, D), 1), HEAD_DIM), 1.0, 0.0)

    def expand(b, carry):
        kx_s[pl.ds(pl.multiple_of(b * HP, HP), HP), :] = (kf_s[pl.ds(b, 1), :] * own_head).astype(BF16)
        return carry

    lax.fori_loop(0, VOCAB, expand, 0)
    scores_of = dot(kx_s[...], qt_s[...], 1, 1)
    upper = scores_of.astype(BF16)
    sc_s[0:VH, :] = upper
    sc_s[VH:2 * VH, :] = (scores_of - upper.astype(F32)).astype(BF16)
    rep = jnp.where(iota((128, 640), 0) == lax.div(iota((128, 640), 1), HP), 1.0, 0.0).astype(BF16)
    head_of = jnp.where(
        lax.div(iota((D, 640), 0), HEAD_DIM) == lax.rem(iota((D, 640), 1), HP), 1.0, 0.0)
    vxt_s[...] = (dot(vf_s[...].T.astype(BF16), rep) * head_of).astype(BF16)
    wm_s[VH:640, :] = jnp.zeros((640 - VH, NCOL * ROWS), BF16)

    row_out.receive()
    fetch[4].wait()
    vo_s[:, part, 0:640] = dot(wro[:, part, :].reshape(4 * 96, D), vxt_s[...]).astype(BF16).reshape(4, 96, 640)
    twin = s + 1 - 2 * core
    row_share = Exchange(
        lambda k: remote(
            vo_s.at[:, part, pl.ds(0, 640)], vo_s.at[:, part, pl.ds(0, 640)], rfs.at[k], rfr.at[k], twin, x),
        lambda k: remote(
            vo_s.at[:, other, pl.ds(0, 640)], vo_s.at[:, other, pl.ds(0, 640)], rfs.at[k], rfr.at[k], twin, x),
        (0,))
    row_share.start()

    ids_y.receive()

    words = idbuf[:, 0, :]
    low = lax.bitwise_and(words, 65535).astype(F32)
    high = lax.shift_right_logical(words, 16).astype(F32)
    table = jnp.concatenate([low[0:64], high[0:64], low[64:128], high[64:128]], axis=0)
    place = iota((ROWS, ROWS), 0)
    from_z = lax.rem(lax.div(place, 128) * 8 + lax.rem(place, 8) + first_z, NZ)
    from_row = lax.rem(lax.div(place, 64), 2) * 128 + lax.rem(lax.div(place, 8), 8) * 16 + from_z
    shuffle = jnp.where(from_row == iota((ROWS, ROWS), 1), 1.0, 0.0).astype(BF16)
    table = dot(shuffle, table.astype(BF16))
    ids = table[:, 0:COLS].astype(BF16)
    live = table[:, COLS:COLS + 128]
    live2 = jnp.concatenate([live, live], axis=1)
    eye = jnp.where(iota((COLS, COLS), 0) == iota((COLS, COLS), 1), 1.0, 0.0).astype(BF16)
    ids_t = dot(eye, ids, 1, 1).astype(BF16)

    def onehot(of, b):
        return jnp.where(of == jnp.asarray(b, BF16), jnp.asarray(1, BF16), jnp.asarray(0, BF16))

    count = jnp.sum(live2, axis=0, keepdims=True)
    first_col = lax.rem(z, 8) * 32 + grp * NCOL
    token = iota((128, ROWS), 0).astype(F32)
    first_lane = jnp.where(iota((128, 128), 1) == 0, 1.0, 0.0).astype(BF16)
    live_row = dot(first_lane, live.astype(BF16), 1, 1)
    own, own_live = [], []
    for i in range(NCOL):
        pick = jnp.where(iota((128, COLS), 1) == first_col + i, 1.0, 0.0).astype(BF16)
        hit = jnp.where(dot(pick, ids, 1, 1) == token, 1.0, 0.0)
        own.append(hit.astype(BF16))
        own_live.append((hit * live_row).astype(BF16))
    wm_s[640:768, :] = jnp.concatenate(own, axis=1)
    picked = dot(sc_s[...], jnp.concatenate(own_live, axis=1)).astype(BF16)
    sums = [None] * 4
    for b in range(VOCAB):
        left = jnp.concatenate([
            picked[at + b * HP:at + (b + 1) * HP, i * ROWS:(i + 1) * ROWS]
            for at in (0, VH) for i in range(NCOL)], axis=0)
        term = dot(left, onehot(ids, b))
        sums[b % 4] = term if sums[b % 4] is None else sums[b % 4] + term
    tied4 = (sums[0] + sums[1]) + (sums[2] + sums[3])
    tied = tied4[0:NCOL * HP] + tied4[NCOL * HP:]
    tied = tied * (HEAD_DIM ** (-0.5) * lax.rsqrt(count))
    top = jnp.max(tied, axis=1, keepdims=True)
    weights = jnp.exp(tied - top)
    probs = (weights / jnp.sum(weights, axis=1, keepdims=True)).astype(BF16)

    for b in range(VOCAB):
        share = dot(probs, onehot(ids_t, b))
        for i in range(NCOL):
            wm_s[b * HP:(b + 1) * HP, i * ROWS:(i + 1) * ROWS] = share[i * HP:(i + 1) * HP].astype(BF16)

    fetch[5].wait()
    row_share.receive()
    col_weight = cqkv_ref[...].reshape(3 * DH, D)
    live_here = live > 0.0

    mixed = dot(vo_s[...].reshape(D, D), wm_s[...])
    near = [mixed[:, i * ROWS:i * ROWS + 128] for i in range(NCOL)]
    for q in range(NX):
        pair = near[q // 2 * 2:q // 2 * 2 + 2]
        at = slice(q % 2 * 64, q % 2 * 64 + 64)
        mixed_s[q] = jnp.concatenate([pair[0][:, at], pair[1][:, at]], axis=1)
    normed2 = norm_cols(mixed).astype(BF16)
    proj = dot(col_weight[DH:], normed2)
    query = dot(col_weight[:DH], jnp.concatenate(
        [normed2[:, i * ROWS:i * ROWS + 128] for i in range(NCOL)], axis=1))
    query = query.astype(BF16) * jnp.asarray(0.125, BF16)
    scores, values = [], []
    for i in range(NCOL):
        at = slice(i * ROWS, (i + 1) * ROWS)
        key = proj[0:DH, at].astype(BF16)
        value = proj[DH:2 * DH, at].astype(BF16)
        for h in range(0, DH, HEAD_DIM):
            scores.append(dot(key[h:h + HEAD_DIM], query[h:h + HEAD_DIM, i * 128:i * 128 + 128], 0, 0))
            values.append(value[h:h + HEAD_DIM])
    weighted, totals = [], []
    for score in scores:
        score = jnp.where(live_here, score, -1e38)
        raw = jnp.exp(score - jnp.max(score, axis=0, keepdims=True))
        totals.append(1.0 / jnp.sum(raw, axis=0, keepdims=True))
        weighted.append(raw.astype(BF16))
    got = [dot(values[q], weighted[q]) * totals[q] for q in range(3 * NCOL)]
    for q in range(NX):
        for h in range(3):
            pair = [got[(q // 2 * 2 + c) * 3 + h][:, q % 2 * 64:q % 2 * 64 + 64] for c in range(2)]
            ctxs[q, h * HEAD_DIM:(h + 1) * HEAD_DIM, :] = jnp.concatenate(pair, axis=1).astype(BF16)
    to_slot = Exchange(
        lambda k: remote(ctxs.at[ahead(k)], ctxr.at[x], xs.at[k], xr.at[k], s, ahead(k)),
        lambda k: remote(ctxs.at[ahead(k)], ctxr.at[behind(k)], xs.at[k], xr.at[k], s, ahead(k)),
        FAR_X)
    to_slot.start()
    col_share = forward(wco, cfs, cfr)
    col_out.receive()
    col_share.start()
    ctxr[x] = ctxs[x]

    fetch[6].wait()
    col_share.receive()
    to_slot.receive()

    context = ctxr[...].reshape(D, 128)

    def a_place(j):
        to_x = lax.rem(x + j // 4, NX)
        to_half = lax.rem(y + (j // 2) % 2, 2)
        return to_x, to_half, lax.rem(core + j % 2, 2)

    def a_out(j):
        to_x, to_half, to_core = a_place(j)
        k = grp * 2 + col_in
        return remote(
            sa.at[j // 4, to_half * 2 + to_core], ra.at[k], as_.at[j], ar.at[k],
            seq_at(2 * half + to_half, z, to_core), to_x)

    def a_into(j):
        from_y = lax.rem(y + j // 4, NY)
        from_core = lax.rem(core + j % 2, 2)
        from_col = lax.rem(col_in + (j // 2) % 2, 2)
        k = (from_y * NC + from_core) * 2 + from_col
        return remote(
            ra.at[k], ra.at[k], as_.at[j], ar.at[k], seq_at(from_y, z, from_core), 2 * from_col + lax.div(y, 2))

    stays = half == lax.div(y, 2)
    to_plane = Exchange(
        a_out, a_into, FAR_PLANE,
        lambda j: jnp.logical_not(stays) if j == 0 else None,
        lambda j: jnp.logical_not(stays) if j == 0 else None)
    for step in (2, 1, 3, 0):
        to_x = lax.rem(x + step, NX)
        rows = pl.ds(pl.multiple_of(to_x * DH, DH), DH)
        turned = (dot(wco[to_x], context) + mixed_s[x, rows, :]).T
        for g in range(4):
            rows_of = [jnp.concatenate([turned[r + g * 8:r + g * 8 + 8], turned[64 + r + g * 8:64 + r + g * 8 + 8]], axis=0)
                       for r in (0, 32)]
            sa[step, g] = jnp.concatenate(rows_of, axis=1).astype(BF16)
        to_plane.start([j for j in FAR_PLANE if j // 4 == step])

    @pl.when(stays)
    def _():
        ra[grp * 2 + col_in] = sa[0, lax.rem(y, 2) * 2 + core]

    order = iota((256, 256), 0)
    swap = jnp.where(lax.rem(order, 32) * 8 + lax.div(order, 32) == iota((256, 256), 1), 1.0, 0.0).astype(BF16)
    to_plane.receive()

    sb[...] = dot(swap, ra[...].reshape(256, 384)).astype(BF16)

    def near_part(step):
        return pl.ds(pl.multiple_of((step + 4 - odd) * 32, 32), 32)

    def col_part(at):
        return pl.ds(pl.multiple_of(lax.rem(at, 8) * 32, 32), 32)

    side = 1 - 2 * odd
    to_rows = Exchange(
        lambda k: remote(
            sb.at[near_part(side * k), :], out_ref.at[col_part(z), :], bs.at[k + 4], br.at[side * k + 4],
            seq_at(y, lax.rem(z + NZ + side * k, NZ), core), x),
        lambda k: remote(
            sb.at[near_part(side * k), :], out_ref.at[col_part(z + NZ - side * k), :], bs.at[k + 4], br.at[side * k + 4],
            seq_at(y, lax.rem(z + NZ + side * k, NZ), core), x),
        NEAR_Z)
    to_rows.start()
    keep = pltpu.make_async_copy(sb.at[near_part(0), :], out_ref.at[col_part(z), :], ls.at[7])
    keep.start()

    ids_z.finish()
    ids_y.finish()
    tabs.finish()
    for weights_sent in (row_out, col_out, row_share, col_share):
        weights_sent.finish()
    to_slot.finish()
    to_plane.finish()
    keep.wait()
    to_rows.finish()
    to_rows.receive()


def body(ids, pad_mask, embed, row_qkv, row_out, col_qkv, col_out):
    dma = pltpu.SemaphoreType.DMA
    got = pl.pallas_call(
        kernel,
        out_shape=pltpu.VMEM((COLS, 2 * DH), BF16),
        in_specs=[pl.BlockSpec(memory_space=pltpu.HBM)] * 7,
        out_specs=pl.BlockSpec(memory_space=pl.ANY),
        scratch_shapes=[
            pltpu.VMEM((2, COLS), jnp.int32),
            pltpu.SMEM((2,), jnp.int32),
            pltpu.VMEM((VOCAB, D), BF16),
            pltpu.VMEM((3, DH, D), BF16),
            pltpu.VMEM((3, DH, D), BF16),
            pltpu.VMEM((128, 1, 384), jnp.int32),
            pltpu.VMEM((NX, 144, 256), BF16),
            pltpu.VMEM((NX, DH, D), BF16),
            pltpu.VMEM((NX, DH, D), BF16),
            pltpu.VMEM((128, D), F32),
            pltpu.VMEM((1024, D), BF16),
            pltpu.VMEM((128, D), BF16),
            pltpu.VMEM((48, D), F32),
            pltpu.VMEM((128, D), F32),
            pltpu.VMEM((VH, D), BF16),
            pltpu.VMEM((D, 640), BF16),
            pltpu.VMEM((D, NCOL * ROWS), BF16),
            pltpu.VMEM((NX, DH, D), BF16),
            pltpu.VMEM((2 * VH, 128), BF16),
            pltpu.VMEM((4, D, 128), F32),
            pltpu.VMEM((NX, DH, 128), BF16),
            pltpu.VMEM((NX, DH, 128), BF16),
            pltpu.VMEM((NX, 4, 16, 384), BF16),
            pltpu.VMEM((16, 16, 384), BF16),
            pltpu.VMEM((256, 384), BF16),
            dma((16,)), dma((16,)),
            dma((8,)), dma((8,)),
            dma((4,)), dma((4,)),
            dma((4,)), dma((4,)), dma((4,)), dma((4,)),
            dma((4,)), dma((4,)), dma((4,)), dma((4,)),
            dma((4,)), dma((4,)),
            dma((16,)), dma((16,)),
            dma((16,)), dma((16,)),
            dma((8,)),
        ],
        compiler_params=pltpu.CompilerParams(
            collective_id=0, has_side_effects=True, vmem_limit_bytes=63 * 1024 * 1024),
        cost_estimate=pl.CostEstimate(flops=6_000_000_000, bytes_accessed=4_000_000, transcendentals=500_000),
        name="msa_layer",
    )(ids, pad_mask, embed, row_qkv, row_out, col_qkv, col_out)
    return jnp.transpose(got.reshape(COLS, 2, DH), (1, 0, 2))


def solution(mesh):
    placed = (
        P("seq", None),
        P("seq"),
        P(),
        P(None, "head", None),
        P("head", None),
        P(None, "head", None),
        P("head", None),
    )
    return jax.shard_map(
        body, mesh=mesh, in_specs=placed, out_specs=P("seq", None, "head"), check_vma=False
    )
```

```python
import jax
import jax.numpy as jnp
from jax import lax
from jax.experimental import pallas as pl
from jax.experimental.pallas import tpu as pltpu
from jax.sharding import PartitionSpec as P

HEAD_DIM = 64
EPS = 1e-05
NX, NY, NZ, NC = 4, 4, 16, 2
VOCAB = 33
D = 768
DH = 192
COLS = 256
ROWS = 256
HP = 16
VH = VOCAB * HP
DIRECT_Z = (4, -4, 3, -3, 2, -2, 1, -1)
FAR_Y = (4, 5, 3, 2, 6, 7, 1)
NEAR_Z = (-4, 3, -3, 2, -2, 1, -1)
NCOL = 4
FAR_X = (2, 1, 3)
FAR_PLANE = (10, 11, 8, 9, 6, 7, 14, 15, 4, 5, 12, 13, 2, 3, 1, 0)
MESH = pl.DeviceIdType.MESH
F32 = jnp.float32
BF16 = jnp.bfloat16


def dot(a, b, ca=1, cb=0):
    return lax.dot_general(a, b, (((ca,), (cb,)), ((), ())), preferred_element_type=F32)


def norm_rows(values):
    mean = jnp.mean(values, axis=1, keepdims=True)
    centred = values - mean
    spread = jnp.mean(centred * centred, axis=1, keepdims=True)
    return centred * lax.rsqrt(spread + EPS)


def norm_cols(values):
    mean = jnp.mean(values, axis=0, keepdims=True)
    centred = values - mean
    spread = jnp.mean(centred * centred, axis=0, keepdims=True)
    return centred * lax.rsqrt(spread + EPS)


def iota(shape, dim):
    return lax.broadcasted_iota(jnp.int32, shape, dim)


class Exchange:
    opened = []

    def __init__(self, out, into, keys, sends=None, arrives=None):
        self.out, self.into, self.keys = out, into, keys
        self.sends = sends or (lambda k: None)
        self.arrives = arrives or (lambda k: None)
        Exchange.opened.append(self)
        self.waited = False

    def each(self, run, keys=None):
        for k in self.keys if keys is None else keys:
            run(k)

    def start(self, keys=None):
        def run(k):
            gate(self.sends(k), lambda: self.out(k).start())
        self.each(run, keys)

    def receive(self, keys=None):
        self.waited = True

        def run(k):
            gate(self.arrives(k), lambda: self.into(k).wait_recv())
        self.each(run, self.keys[::-1] if keys is None else keys)

    def finish(self):
        def run(k):
            gate(self.sends(k), lambda: self.out(k).wait_send())
        self.each(run)


def gate(condition, action):
    if condition is None:
        action()
    else:
        pl.when(condition)(action)


def kernel(
    ids_hbm, mask_hbm, embed_hbm, rqkv_hbm, rout_hbm, cqkv_hbm, cout_hbm,
    out_ref,
    ids_ref, mask_ref, embed_ref, rqkv_ref, cqkv_ref,
    idbuf, tab, wro, wco, emb_s, sel_s, qt_s, kf_s, vf_s, kx_s, vxt_s, wm_s, vo_s, sc_s,
    mixed_s, ctxs, ctxr, sa, ra, sb,
    zs, zr, ys, yr, ts, tr, ros, ror, rfs, rfr, cos, cor, cfs, cfr, xs, xr, as_, ar, bs, br, ls,
):
    Exchange.opened = []
    s = lax.axis_index("seq")
    x = lax.axis_index("head")
    y = lax.div(s, NZ * NC)
    z = lax.rem(lax.div(s, NC), NZ)
    core = lax.rem(s, NC)
    grp = y * NC + core
    half = lax.rem(x, 2)
    col_in = lax.div(x, 2)
    odd = lax.rem(z, 2)
    first_z = lax.rem(z + NZ - 4 + odd, NZ)

    def seq_at(yy, zz, cc):
        return (yy * NZ + zz) * NC + cc

    def remote(src, dst, ss, rs, to_s, to_x):
        return pltpu.make_async_remote_copy(
            src_ref=src, dst_ref=dst, send_sem=ss, recv_sem=rs, device_id=(to_s, to_x), device_id_type=MESH)

    barrier = pltpu.get_barrier_semaphore()

    for k in DIRECT_Z:
        pl.semaphore_signal(
            barrier, inc=1, device_id=(seq_at(y, lax.rem(z + NZ + k, NZ), core), x), device_id_type=MESH)

    def greet_plane(k, carry):
        place = lax.rem(x * 8 + grp + k, 32)
        px, pg = lax.div(place, 8), lax.rem(place, 8)
        pl.semaphore_signal(
            barrier, inc=1, device_id=(seq_at(lax.div(pg, NC), z, lax.rem(pg, NC)), px), device_id_type=MESH)
        return carry

    lax.fori_loop(1, 32, greet_plane, 0)
    fetch = [
        pltpu.make_async_copy(a, b, ls.at[i]) for i, (a, b) in enumerate((
            (ids_hbm, ids_ref), (mask_hbm, mask_ref), (embed_hbm, embed_ref), (rqkv_hbm, rqkv_ref),
            (rout_hbm, wro.at[x]), (cqkv_hbm, cqkv_ref), (cout_hbm, wco.at[x])))
    ]
    for copy in fetch:
        copy.start()

    slot = grp * NZ + z
    fetch[0].wait()
    fetch[1].wait()
    m0 = mask_ref[0]
    m1 = mask_ref[1]
    idbuf[slot, :, 0:COLS] = ids_ref[0:1, :] + ids_ref[1:2, :] * 65536
    idbuf[slot, :, COLS:COLS + 128] = jnp.zeros((1, 128), jnp.int32) + (m0 + m1 * 65536)

    pl.semaphore_wait(barrier, len(DIRECT_Z) + 31)

    def z_slot(k):
        return idbuf.at[grp * NZ + lax.rem(z + NZ + k, NZ)]

    def z_seq(k):
        return seq_at(y, lax.rem(z + NZ + k, NZ), core)

    ids_z = Exchange(
        lambda k: remote(z_slot(0), z_slot(0), zs.at[k + 4], zr.at[k + 4], z_seq(k), x),
        lambda k: remote(z_slot(-k), z_slot(-k), zs.at[k + 4], zr.at[k + 4], z_seq(k), x),
        DIRECT_Z)
    ids_down = Exchange(
        lambda k: remote(z_slot(k), z_slot(k), zs.at[8 + k], zr.at[8 + k], z_seq(-4), x),
        lambda k: remote(z_slot(4 + k), z_slot(4 + k), zs.at[8 + k], zr.at[8 + k], z_seq(-4), x),
        (4, 3, 2, 1))
    ids_up = Exchange(
        lambda k: remote(z_slot(-k), z_slot(-k), zs.at[12 + k], zr.at[12 + k], z_seq(4), x),
        lambda k: remote(z_slot(-4 - k), z_slot(-4 - k), zs.at[12 + k], zr.at[12 + k], z_seq(4), x),
        (3, 2, 1))
    ids_z.start()

    fetch[2].wait()
    emb_s[...] = jnp.zeros_like(emb_s)
    emb_s[0:VOCAB, :] = embed_ref[...].astype(F32)
    normed = norm_rows(emb_s[...]).astype(BF16)[0:48, :]
    tab[x] = jnp.zeros((144, 256), BF16)
    fetch[3].wait()
    for t in range(3):
        tab[x, t * 48:(t + 1) * 48, 0:DH] = dot(normed, rqkv_ref[t], 1, 1).astype(BF16)

    part = pl.ds(pl.multiple_of(core * 96, 96), 96)
    other = pl.ds(pl.multiple_of((1 - core) * 96, 96), 96)
    ahead = lambda k: lax.rem(x + k, NX)
    behind = lambda k: lax.rem(x + NX - k, NX)

    def weight(src, buf, ss, rs):
        return Exchange(
            lambda k: remote(src.at[part, :], buf.at[x, part, :], ss.at[k], rs.at[k], s, ahead(k)),
            lambda k: remote(src.at[part, :], buf.at[behind(k), part, :], ss.at[k], rs.at[k], s, ahead(k)),
            FAR_X)

    def forward(buf, ss, rs):
        twin = s + 1 - 2 * core
        return Exchange(
            lambda k: remote(
                buf.at[behind(k), part, :], buf.at[behind(k), part, :], ss.at[k], rs.at[k], twin, x),
            lambda k: remote(
                buf.at[behind(k), other, :], buf.at[behind(k), other, :], ss.at[k], rs.at[k], twin, x),
            FAR_X)

    tabs = Exchange(
        lambda k: remote(tab.at[x], tab.at[x], ts.at[k], tr.at[k], s, ahead(k)),
        lambda k: remote(tab.at[behind(k)], tab.at[behind(k)], ts.at[k], tr.at[k], s, ahead(k)),
        FAR_X)
    tabs.start()
    row_out = weight(rout_hbm, wro, ros, ror)
    row_out.start()
    col_out = weight(cout_hbm, wco, cos, cor)

    vo_s[:, :, 640:768] = emb_s[...].T.astype(BF16).reshape(NX, DH, 128)
    spot = iota((4 * 256, D), 0)
    goal = lax.div(spot, 256) * DH + lax.rem(spot, 256)
    sel_s[...] = jnp.where(
        jnp.logical_and(goal == iota((4 * 256, D), 1), lax.rem(spot, 256) < DH), 1.0, 0.0).astype(BF16)

    ids_z.receive((1, 2, 3))
    ids_up.start()
    ids_z.receive((-1, -2, -3, -4))
    ids_down.start()
    ids_z.receive((4,))
    ids_up.receive()
    ids_down.receive()
    mine = pl.ds(grp * NZ, NZ)

    def y_seq(k):
        to = lax.rem(grp + k, 8)
        return seq_at(lax.div(to, NC), z, lax.rem(to, NC))

    def y_part(k):
        return idbuf.at[pl.ds(lax.rem(grp + 8 - k, 8) * NZ, NZ)]

    ids_y = Exchange(
        lambda k: remote(idbuf.at[mine], idbuf.at[mine], ys.at[k], yr.at[k], y_seq(k), x),
        lambda k: remote(y_part(k), y_part(k), ys.at[k], yr.at[k], y_seq(k), x),
        FAR_Y)
    ids_y.start()
    col_out.start()

    tabs.receive()
    gathered = jnp.concatenate([tab[i] for i in range(NX)], axis=1)
    tables = dot(gathered, sel_s[...])
    qt_s[...] = jnp.zeros_like(qt_s)
    qt_s[0:48, :] = tables[0:48].astype(BF16)
    kf_s[...] = tables[48:96]
    vf_s[...] = jnp.zeros_like(vf_s)
    vf_s[0:48, :] = tables[96:144]
    own_head = jnp.where(iota((HP, D), 0) == lax.div(iota((HP, D), 1), HEAD_DIM), 1.0, 0.0)

    def expand(b, carry):
        kx_s[pl.ds(pl.multiple_of(b * HP, HP), HP), :] = (kf_s[pl.ds(b, 1), :] * own_head).astype(BF16)
        return carry

    lax.fori_loop(0, VOCAB, expand, 0)
    scores_of = dot(kx_s[...], qt_s[...], 1, 1)
    upper = scores_of.astype(BF16)
    sc_s[0:VH, :] = upper
    sc_s[VH:2 * VH, :] = (scores_of - upper.astype(F32)).astype(BF16)
    rep = jnp.where(iota((128, 640), 0) == lax.div(iota((128, 640), 1), HP), 1.0, 0.0).astype(BF16)
    head_of = jnp.where(
        lax.div(iota((D, 640), 0), HEAD_DIM) == lax.rem(iota((D, 640), 1), HP), 1.0, 0.0)
    vxt_s[...] = (dot(vf_s[...].T.astype(BF16), rep) * head_of).astype(BF16)
    wm_s[VH:640, :] = jnp.zeros((640 - VH, NCOL * ROWS), BF16)

    row_out.receive()
    fetch[4].wait()
    vo_s[:, part, 0:640] = dot(wro[:, part, :].reshape(4 * 96, D), vxt_s[...]).astype(BF16).reshape(4, 96, 640)
    twin = s + 1 - 2 * core
    row_share = Exchange(
        lambda k: remote(
            vo_s.at[:, part, pl.ds(0, 640)], vo_s.at[:, part, pl.ds(0, 640)], rfs.at[k], rfr.at[k], twin, x),
        lambda k: remote(
            vo_s.at[:, other, pl.ds(0, 640)], vo_s.at[:, other, pl.ds(0, 640)], rfs.at[k], rfr.at[k], twin, x),
        (0,))
    row_share.start()

    ids_y.receive()

    words = idbuf[:, 0, :]
    low = lax.bitwise_and(words, 65535).astype(F32)
    high = lax.shift_right_logical(words, 16).astype(F32)
    table = jnp.concatenate([low[0:64], high[0:64], low[64:128], high[64:128]], axis=0)
    place = iota((ROWS, ROWS), 0)
    from_z = lax.rem(lax.div(place, 128) * 8 + lax.rem(place, 8) + first_z, NZ)
    from_row = lax.rem(lax.div(place, 64), 2) * 128 + lax.rem(lax.div(place, 8), 8) * 16 + from_z
    shuffle = jnp.where(from_row == iota((ROWS, ROWS), 1), 1.0, 0.0).astype(BF16)
    table = dot(shuffle, table.astype(BF16))
    ids = table[:, 0:COLS].astype(BF16)
    live = table[:, COLS:COLS + 128]
    live2 = jnp.concatenate([live, live], axis=1)
    eye = jnp.where(iota((COLS, COLS), 0) == iota((COLS, COLS), 1), 1.0, 0.0).astype(BF16)
    ids_t = dot(eye, ids, 1, 1).astype(BF16)

    def onehot(of, b):
        return jnp.where(of == jnp.asarray(b, BF16), jnp.asarray(1, BF16), jnp.asarray(0, BF16))

    count = jnp.sum(live2, axis=0, keepdims=True)
    first_col = lax.rem(z, 8) * 32 + grp * NCOL
    token = iota((128, ROWS), 0).astype(F32)
    first_lane = jnp.where(iota((128, 128), 1) == 0, 1.0, 0.0).astype(BF16)
    live_row = dot(first_lane, live.astype(BF16), 1, 1)
    own, own_live = [], []
    for i in range(NCOL):
        pick = jnp.where(iota((128, COLS), 1) == first_col + i, 1.0, 0.0).astype(BF16)
        hit = jnp.where(dot(pick, ids, 1, 1) == token, 1.0, 0.0)
        own.append(hit.astype(BF16))
        own_live.append((hit * live_row).astype(BF16))
    wm_s[640:768, :] = jnp.concatenate(own, axis=1)
    picked = dot(sc_s[...], jnp.concatenate(own_live, axis=1)).astype(BF16)
    sums = [None] * 4
    for b in range(VOCAB):
        left = jnp.concatenate([
            picked[at + b * HP:at + (b + 1) * HP, i * ROWS:(i + 1) * ROWS]
            for at in (0, VH) for i in range(NCOL)], axis=0)
        term = dot(left, onehot(ids, b))
        sums[b % 4] = term if sums[b % 4] is None else sums[b % 4] + term
    tied4 = (sums[0] + sums[1]) + (sums[2] + sums[3])
    tied = tied4[0:NCOL * HP] + tied4[NCOL * HP:]
    tied = tied * (HEAD_DIM ** (-0.5) * lax.rsqrt(count))
    top = jnp.max(tied, axis=1, keepdims=True)
    weights = jnp.exp(tied - top)
    scale = 1.0 / jnp.sum(weights, axis=1, keepdims=True)
    weights = weights.astype(BF16)

    for b in range(VOCAB):
        share = dot(weights, onehot(ids_t, b)) * scale
        for i in range(NCOL):
            wm_s[b * HP:(b + 1) * HP, i * ROWS:(i + 1) * ROWS] = share[i * HP:(i + 1) * HP].astype(BF16)

    fetch[5].wait()
    row_share.receive()
    col_weight = cqkv_ref[...].reshape(3 * DH, D)
    live_here = live > 0.0

    mixed = dot(vo_s[...].reshape(D, D), wm_s[...])
    near = [mixed[:, i * ROWS:i * ROWS + 128] for i in range(NCOL)]
    for q in range(NX):
        pair = near[q // 2 * 2:q // 2 * 2 + 2]
        at = slice(q % 2 * 64, q % 2 * 64 + 64)
        mixed_s[q] = jnp.concatenate([pair[0][:, at], pair[1][:, at]], axis=1)
    normed2 = norm_cols(mixed).astype(BF16)
    proj = dot(col_weight[DH:], normed2)
    query = dot(col_weight[:DH], jnp.concatenate(
        [normed2[:, i * ROWS:i * ROWS + 128] for i in range(NCOL)], axis=1))
    query = query.astype(BF16) * jnp.asarray(0.125, BF16)
    scores, values = [], []
    for i in range(NCOL):
        at = slice(i * ROWS, (i + 1) * ROWS)
        key = proj[0:DH, at].astype(BF16)
        value = proj[DH:2 * DH, at].astype(BF16)
        for h in range(0, DH, HEAD_DIM):
            scores.append(dot(key[h:h + HEAD_DIM], query[h:h + HEAD_DIM, i * 128:i * 128 + 128], 0, 0))
            values.append(value[h:h + HEAD_DIM])
    weighted, totals = [], []
    for score in scores:
        score = jnp.where(live_here, score, -1e38)
        raw = jnp.exp(score - jnp.max(score, axis=0, keepdims=True))
        totals.append(1.0 / jnp.sum(raw, axis=0, keepdims=True))
        weighted.append(raw.astype(BF16))
    got = [dot(values[q], weighted[q]) * totals[q] for q in range(3 * NCOL)]
    for q in range(NX):
        for h in range(3):
            pair = [got[(q // 2 * 2 + c) * 3 + h][:, q % 2 * 64:q % 2 * 64 + 64] for c in range(2)]
            ctxs[q, h * HEAD_DIM:(h + 1) * HEAD_DIM, :] = jnp.concatenate(pair, axis=1).astype(BF16)
    to_slot = Exchange(
        lambda k: remote(ctxs.at[ahead(k)], ctxr.at[x], xs.at[k], xr.at[k], s, ahead(k)),
        lambda k: remote(ctxs.at[ahead(k)], ctxr.at[behind(k)], xs.at[k], xr.at[k], s, ahead(k)),
        FAR_X)
    to_slot.start()
    col_share = forward(wco, cfs, cfr)
    col_out.receive()
    col_share.start()
    ctxr[x] = ctxs[x]

    fetch[6].wait()
    col_share.receive()
    to_slot.receive()

    context = ctxr[...].reshape(D, 128)

    def a_place(j):
        to_x = lax.rem(x + j // 4, NX)
        to_half = lax.rem(y + (j // 2) % 2, 2)
        return to_x, to_half, lax.rem(core + j % 2, 2)

    def a_out(j):
        to_x, to_half, to_core = a_place(j)
        k = grp * 2 + col_in
        return remote(
            sa.at[j // 4, to_half * 2 + to_core], ra.at[k], as_.at[j], ar.at[k],
            seq_at(2 * half + to_half, z, to_core), to_x)

    def a_into(j):
        from_y = lax.rem(y + j // 4, NY)
        from_core = lax.rem(core + j % 2, 2)
        from_col = lax.rem(col_in + (j // 2) % 2, 2)
        k = (from_y * NC + from_core) * 2 + from_col
        return remote(
            ra.at[k], ra.at[k], as_.at[j], ar.at[k], seq_at(from_y, z, from_core), 2 * from_col + lax.div(y, 2))

    stays = half == lax.div(y, 2)
    to_plane = Exchange(
        a_out, a_into, FAR_PLANE,
        lambda j: jnp.logical_not(stays) if j == 0 else None,
        lambda j: jnp.logical_not(stays) if j == 0 else None)
    for step in (2, 1, 3, 0):
        to_x = lax.rem(x + step, NX)
        rows = pl.ds(pl.multiple_of(to_x * DH, DH), DH)
        turned = (dot(wco[to_x], context) + mixed_s[x, rows, :]).T
        for g in range(4):
            rows_of = [jnp.concatenate([turned[r + g * 8:r + g * 8 + 8], turned[64 + r + g * 8:64 + r + g * 8 + 8]], axis=0)
                       for r in (0, 32)]
            sa[step, g] = jnp.concatenate(rows_of, axis=1).astype(BF16)
        to_plane.start([j for j in FAR_PLANE if j // 4 == step])

    @pl.when(stays)
    def _():
        ra[grp * 2 + col_in] = sa[0, lax.rem(y, 2) * 2 + core]

    order = iota((256, 256), 0)
    swap = jnp.where(lax.rem(order, 32) * 8 + lax.div(order, 32) == iota((256, 256), 1), 1.0, 0.0).astype(BF16)
    to_plane.receive()

    sb[...] = dot(swap, ra[...].reshape(256, 384)).astype(BF16)

    def near_part(step):
        return pl.ds(pl.multiple_of((step + 4 - odd) * 32, 32), 32)

    def col_part(at):
        return pl.ds(pl.multiple_of(lax.rem(at, 8) * 32, 32), 32)

    side = 1 - 2 * odd
    to_rows = Exchange(
        lambda k: remote(
            sb.at[near_part(side * k), :], out_ref.at[col_part(z), :], bs.at[k + 4], br.at[side * k + 4],
            seq_at(y, lax.rem(z + NZ + side * k, NZ), core), x),
        lambda k: remote(
            sb.at[near_part(side * k), :], out_ref.at[col_part(z + NZ - side * k), :], bs.at[k + 4], br.at[side * k + 4],
            seq_at(y, lax.rem(z + NZ + side * k, NZ), core), x),
        NEAR_Z)
    to_rows.start()
    keep = pltpu.make_async_copy(sb.at[near_part(0), :], out_ref.at[col_part(z), :], ls.at[7])
    keep.start()

    ids_z.finish()
    ids_up.finish()
    ids_down.finish()
    ids_y.finish()
    tabs.finish()
    for weights_sent in (row_out, col_out, row_share, col_share):
        weights_sent.finish()
    to_slot.finish()
    to_plane.finish()
    keep.wait()
    to_rows.finish()
    to_rows.receive()


def body(ids, pad_mask, embed, row_qkv, row_out, col_qkv, col_out):
    dma = pltpu.SemaphoreType.DMA
    got = pl.pallas_call(
        kernel,
        out_shape=pltpu.VMEM((COLS, 2 * DH), BF16),
        in_specs=[pl.BlockSpec(memory_space=pltpu.HBM)] * 7,
        out_specs=pl.BlockSpec(memory_space=pl.ANY),
        scratch_shapes=[
            pltpu.VMEM((2, COLS), jnp.int32),
            pltpu.SMEM((2,), jnp.int32),
            pltpu.VMEM((VOCAB, D), BF16),
            pltpu.VMEM((3, DH, D), BF16),
            pltpu.VMEM((3, DH, D), BF16),
            pltpu.VMEM((128, 1, 384), jnp.int32),
            pltpu.VMEM((NX, 144, 256), BF16),
            pltpu.VMEM((NX, DH, D), BF16),
            pltpu.VMEM((NX, DH, D), BF16),
            pltpu.VMEM((128, D), F32),
            pltpu.VMEM((1024, D), BF16),
            pltpu.VMEM((128, D), BF16),
            pltpu.VMEM((48, D), F32),
            pltpu.VMEM((128, D), F32),
            pltpu.VMEM((VH, D), BF16),
            pltpu.VMEM((D, 640), BF16),
            pltpu.VMEM((D, NCOL * ROWS), BF16),
            pltpu.VMEM((NX, DH, D), BF16),
            pltpu.VMEM((2 * VH, 128), BF16),
            pltpu.VMEM((4, D, 128), F32),
            pltpu.VMEM((NX, DH, 128), BF16),
            pltpu.VMEM((NX, DH, 128), BF16),
            pltpu.VMEM((NX, 4, 16, 384), BF16),
            pltpu.VMEM((16, 16, 384), BF16),
            pltpu.VMEM((256, 384), BF16),
            dma((16,)), dma((16,)),
            dma((8,)), dma((8,)),
            dma((4,)), dma((4,)),
            dma((4,)), dma((4,)), dma((4,)), dma((4,)),
            dma((4,)), dma((4,)), dma((4,)), dma((4,)),
            dma((4,)), dma((4,)),
            dma((16,)), dma((16,)),
            dma((16,)), dma((16,)),
            dma((8,)),
        ],
        compiler_params=pltpu.CompilerParams(
            collective_id=0, has_side_effects=True, vmem_limit_bytes=63 * 1024 * 1024),
        cost_estimate=pl.CostEstimate(flops=6_000_000_000, bytes_accessed=4_000_000, transcendentals=500_000),
        name="msa_layer",
    )(ids, pad_mask, embed, row_qkv, row_out, col_qkv, col_out)
    return jnp.transpose(got.reshape(COLS, 2, DH), (1, 0, 2))


def solution(mesh):
    placed = (
        P("seq", None),
        P("seq"),
        P(),
        P(None, "head", None),
        P("head", None),
        P(None, "head", None),
        P("head", None),
    )
    return jax.shard_map(
        body, mesh=mesh, in_specs=placed, out_specs=P("seq", None, "head"), check_vma=False
    )
```

```python
import jax
import jax.numpy as jnp
from jax import lax
from jax.experimental import pallas as pl
from jax.experimental.pallas import tpu as pltpu
from jax.sharding import PartitionSpec as P

HEAD_DIM = 64
EPS = 1e-05
NX, NY, NZ, NC = 4, 4, 16, 2
VOCAB = 33
D = 768
DH = 192
COLS = 256
ROWS = 256
HP = 16
VH = VOCAB * HP
DIRECT_Z = (4, -4, 3, -3, 2, -2, 1, -1)
FAR_Y = (4, 5, 3, 2, 6, 7, 1)
NEAR_Z = (-4, 3, -3, 2, -2, 1, -1)
NCOL = 4
FAR_X = (2, 1, 3)
FAR_PLANE = (10, 11, 8, 9, 6, 7, 14, 15, 4, 5, 12, 13, 2, 3, 1, 0)
MESH = pl.DeviceIdType.MESH
F32 = jnp.float32
BF16 = jnp.bfloat16


def dot(a, b, ca=1, cb=0):
    return lax.dot_general(a, b, (((ca,), (cb,)), ((), ())), preferred_element_type=F32)


def norm_rows(values):
    mean = jnp.mean(values, axis=1, keepdims=True)
    centred = values - mean
    spread = jnp.mean(centred * centred, axis=1, keepdims=True)
    return centred * lax.rsqrt(spread + EPS)


def norm_cols(values):
    mean = jnp.mean(values, axis=0, keepdims=True)
    centred = values - mean
    spread = jnp.mean(centred * centred, axis=0, keepdims=True)
    return centred * lax.rsqrt(spread + EPS)


def iota(shape, dim):
    return lax.broadcasted_iota(jnp.int32, shape, dim)


class Exchange:
    opened = []

    def __init__(self, out, into, keys, sends=None, arrives=None):
        self.out, self.into, self.keys = out, into, keys
        self.sends = sends or (lambda k: None)
        self.arrives = arrives or (lambda k: None)
        Exchange.opened.append(self)
        self.waited = False

    def each(self, run, keys=None):
        for k in self.keys if keys is None else keys:
            run(k)

    def start(self, keys=None):
        def run(k):
            gate(self.sends(k), lambda: self.out(k).start())
        self.each(run, keys)

    def receive(self, keys=None):
        self.waited = True

        def run(k):
            gate(self.arrives(k), lambda: self.into(k).wait_recv())
        self.each(run, self.keys[::-1] if keys is None else keys)

    def finish(self):
        def run(k):
            gate(self.sends(k), lambda: self.out(k).wait_send())
        self.each(run)


def gate(condition, action):
    if condition is None:
        action()
    else:
        pl.when(condition)(action)


def kernel(
    ids_hbm, mask_hbm, embed_hbm, rqkv_hbm, rout_hbm, cqkv_hbm, cout_hbm,
    out_ref,
    ids_ref, mask_ref, embed_ref, rqkv_ref, cqkv_ref,
    idbuf, tab, wro, wco, emb_s, sel_s, qt_s, kf_s, vf_s, kx_s, vxt_s, wm_s, vo_s, sc_s,
    mixed_s, ctxs, ctxr, sa, ra, sb,
    zs, zr, ys, yr, ts, tr, ros, ror, rfs, rfr, cos, cor, cfs, cfr, xs, xr, as_, ar, bs, br, ls,
):
    Exchange.opened = []
    s = lax.axis_index("seq")
    x = lax.axis_index("head")
    y = lax.div(s, NZ * NC)
    z = lax.rem(lax.div(s, NC), NZ)
    core = lax.rem(s, NC)
    grp = y * NC + core
    half = lax.rem(x, 2)
    col_in = lax.div(x, 2)
    odd = lax.rem(z, 2)
    first_z = lax.rem(z + NZ - 4 + odd, NZ)

    def seq_at(yy, zz, cc):
        return (yy * NZ + zz) * NC + cc

    def remote(src, dst, ss, rs, to_s, to_x):
        return pltpu.make_async_remote_copy(
            src_ref=src, dst_ref=dst, send_sem=ss, recv_sem=rs, device_id=(to_s, to_x), device_id_type=MESH)

    fetch = [
        pltpu.make_async_copy(a, b, ls.at[i]) for i, (a, b) in enumerate((
            (ids_hbm, ids_ref), (mask_hbm, mask_ref), (embed_hbm, embed_ref), (rqkv_hbm, rqkv_ref),
            (rout_hbm, wro.at[x]), (cqkv_hbm, cqkv_ref), (cout_hbm, wco.at[x])))
    ]
    fetch[0].start()
    fetch[1].start()
    barrier = pltpu.get_barrier_semaphore()

    for k in DIRECT_Z:
        pl.semaphore_signal(
            barrier, inc=1, device_id=(seq_at(y, lax.rem(z + NZ + k, NZ), core), x), device_id_type=MESH)

    def greet_plane(k, carry):
        place = lax.rem(x * 8 + grp + k, 32)
        px, pg = lax.div(place, 8), lax.rem(place, 8)
        pl.semaphore_signal(
            barrier, inc=1, device_id=(seq_at(lax.div(pg, NC), z, lax.rem(pg, NC)), px), device_id_type=MESH)
        return carry

    lax.fori_loop(1, 32, greet_plane, 0)
    for copy in fetch[2:]:
        copy.start()

    slot = grp * NZ + z
    fetch[0].wait()
    fetch[1].wait()
    m0 = mask_ref[0]
    m1 = mask_ref[1]
    idbuf[slot, :, 0:COLS] = ids_ref[0:1, :] + ids_ref[1:2, :] * 65536
    idbuf[slot, :, COLS:COLS + 128] = jnp.zeros((1, 128), jnp.int32) + (m0 + m1 * 65536)

    pl.semaphore_wait(barrier, len(DIRECT_Z) + 31)

    def z_slot(k):
        return idbuf.at[grp * NZ + lax.rem(z + NZ + k, NZ)]

    def z_seq(k):
        return seq_at(y, lax.rem(z + NZ + k, NZ), core)

    ids_z = Exchange(
        lambda k: remote(z_slot(0), z_slot(0), zs.at[k + 4], zr.at[k + 4], z_seq(k), x),
        lambda k: remote(z_slot(-k), z_slot(-k), zs.at[k + 4], zr.at[k + 4], z_seq(k), x),
        DIRECT_Z)
    ids_down = Exchange(
        lambda k: remote(z_slot(k), z_slot(k), zs.at[8 + k], zr.at[8 + k], z_seq(-4), x),
        lambda k: remote(z_slot(4 + k), z_slot(4 + k), zs.at[8 + k], zr.at[8 + k], z_seq(-4), x),
        (4, 3, 2, 1))
    ids_up = Exchange(
        lambda k: remote(z_slot(-k), z_slot(-k), zs.at[12 + k], zr.at[12 + k], z_seq(4), x),
        lambda k: remote(z_slot(-4 - k), z_slot(-4 - k), zs.at[12 + k], zr.at[12 + k], z_seq(4), x),
        (3, 2, 1))
    ids_z.start()

    fetch[2].wait()
    emb_s[...] = jnp.zeros_like(emb_s)
    emb_s[0:VOCAB, :] = embed_ref[...].astype(F32)
    normed = norm_rows(emb_s[...]).astype(BF16)[0:48, :]
    tab[x] = jnp.zeros((144, 256), BF16)
    fetch[3].wait()
    for t in range(3):
        tab[x, t * 48:(t + 1) * 48, 0:DH] = dot(normed, rqkv_ref[t], 1, 1).astype(BF16)

    part = pl.ds(pl.multiple_of(core * 96, 96), 96)
    other = pl.ds(pl.multiple_of((1 - core) * 96, 96), 96)
    ahead = lambda k: lax.rem(x + k, NX)
    behind = lambda k: lax.rem(x + NX - k, NX)

    def weight(src, buf, ss, rs):
        return Exchange(
            lambda k: remote(src.at[part, :], buf.at[x, part, :], ss.at[k], rs.at[k], s, ahead(k)),
            lambda k: remote(src.at[part, :], buf.at[behind(k), part, :], ss.at[k], rs.at[k], s, ahead(k)),
            FAR_X)

    def forward(buf, ss, rs):
        twin = s + 1 - 2 * core
        return Exchange(
            lambda k: remote(
                buf.at[behind(k), part, :], buf.at[behind(k), part, :], ss.at[k], rs.at[k], twin, x),
            lambda k: remote(
                buf.at[behind(k), other, :], buf.at[behind(k), other, :], ss.at[k], rs.at[k], twin, x),
            FAR_X)

    tabs = Exchange(
        lambda k: remote(tab.at[x], tab.at[x], ts.at[k], tr.at[k], s, ahead(k)),
        lambda k: remote(tab.at[behind(k)], tab.at[behind(k)], ts.at[k], tr.at[k], s, ahead(k)),
        FAR_X)
    tabs.start()
    row_out = weight(rout_hbm, wro, ros, ror)
    row_out.start()
    col_out = weight(cout_hbm, wco, cos, cor)

    vo_s[:, :, 640:768] = emb_s[...].T.astype(BF16).reshape(NX, DH, 128)
    spot = iota((4 * 256, D), 0)
    goal = lax.div(spot, 256) * DH + lax.rem(spot, 256)
    sel_s[...] = jnp.where(
        jnp.logical_and(goal == iota((4 * 256, D), 1), lax.rem(spot, 256) < DH), 1.0, 0.0).astype(BF16)

    ids_z.receive((1, 2, 3))
    ids_up.start()
    ids_z.receive((-1, -2, -3, -4))
    ids_down.start()
    ids_z.receive((4,))
    ids_up.receive()
    ids_down.receive()
    mine = pl.ds(grp * NZ, NZ)

    def y_seq(k):
        to = lax.rem(grp + k, 8)
        return seq_at(lax.div(to, NC), z, lax.rem(to, NC))

    def y_part(k):
        return idbuf.at[pl.ds(lax.rem(grp + 8 - k, 8) * NZ, NZ)]

    ids_y = Exchange(
        lambda k: remote(idbuf.at[mine], idbuf.at[mine], ys.at[k], yr.at[k], y_seq(k), x),
        lambda k: remote(y_part(k), y_part(k), ys.at[k], yr.at[k], y_seq(k), x),
        FAR_Y)
    ids_y.start()
    col_out.start()

    tabs.receive()
    gathered = jnp.concatenate([tab[i] for i in range(NX)], axis=1)
    tables = dot(gathered, sel_s[...])
    qt_s[...] = jnp.zeros_like(qt_s)
    qt_s[0:48, :] = tables[0:48].astype(BF16)
    kf_s[...] = tables[48:96]
    vf_s[...] = jnp.zeros_like(vf_s)
    vf_s[0:48, :] = tables[96:144]
    own_head = jnp.where(iota((HP, D), 0) == lax.div(iota((HP, D), 1), HEAD_DIM), 1.0, 0.0)

    def expand(b, carry):
        kx_s[pl.ds(pl.multiple_of(b * HP, HP), HP), :] = (kf_s[pl.ds(b, 1), :] * own_head).astype(BF16)
        return carry

    lax.fori_loop(0, VOCAB, expand, 0)
    scores_of = dot(kx_s[...], qt_s[...], 1, 1)
    upper = scores_of.astype(BF16)
    sc_s[0:VH, :] = upper
    sc_s[VH:2 * VH, :] = (scores_of - upper.astype(F32)).astype(BF16)
    rep = jnp.where(iota((128, 640), 0) == lax.div(iota((128, 640), 1), HP), 1.0, 0.0).astype(BF16)
    head_of = jnp.where(
        lax.div(iota((D, 640), 0), HEAD_DIM) == lax.rem(iota((D, 640), 1), HP), 1.0, 0.0)
    vxt_s[...] = (dot(vf_s[...].T.astype(BF16), rep) * head_of).astype(BF16)
    wm_s[VH:640, :] = jnp.zeros((640 - VH, NCOL * ROWS), BF16)

    row_out.receive()
    fetch[4].wait()
    vo_s[:, part, 0:640] = dot(wro[:, part, :].reshape(4 * 96, D), vxt_s[...]).astype(BF16).reshape(4, 96, 640)
    twin = s + 1 - 2 * core
    row_share = Exchange(
        lambda k: remote(
            vo_s.at[:, part, pl.ds(0, 640)], vo_s.at[:, part, pl.ds(0, 640)], rfs.at[k], rfr.at[k], twin, x),
        lambda k: remote(
            vo_s.at[:, other, pl.ds(0, 640)], vo_s.at[:, other, pl.ds(0, 640)], rfs.at[k], rfr.at[k], twin, x),
        (0,))
    row_share.start()

    ids_y.receive()

    words = idbuf[:, 0, :]
    low = lax.bitwise_and(words, 65535).astype(F32)
    high = lax.shift_right_logical(words, 16).astype(F32)
    table = jnp.concatenate([low[0:64], high[0:64], low[64:128], high[64:128]], axis=0)
    place = iota((ROWS, ROWS), 0)
    from_z = lax.rem(lax.div(place, 128) * 8 + lax.rem(place, 8) + first_z, NZ)
    from_row = lax.rem(lax.div(place, 64), 2) * 128 + lax.rem(lax.div(place, 8), 8) * 16 + from_z
    shuffle = jnp.where(from_row == iota((ROWS, ROWS), 1), 1.0, 0.0).astype(BF16)
    table = dot(shuffle, table.astype(BF16))
    ids = table[:, 0:COLS].astype(BF16)
    live = table[:, COLS:COLS + 128]
    live2 = jnp.concatenate([live, live], axis=1)
    eye = jnp.where(iota((COLS, COLS), 0) == iota((COLS, COLS), 1), 1.0, 0.0).astype(BF16)
    ids_t = dot(eye, ids, 1, 1).astype(BF16)

    def onehot(of, b):
        return jnp.where(of == jnp.asarray(b, BF16), jnp.asarray(1, BF16), jnp.asarray(0, BF16))

    count = jnp.sum(live2, axis=0, keepdims=True)
    first_col = lax.rem(z, 8) * 32 + grp * NCOL
    token = iota((128, ROWS), 0).astype(F32)
    first_lane = jnp.where(iota((128, 128), 1) == 0, 1.0, 0.0).astype(BF16)
    live_row = dot(first_lane, live.astype(BF16), 1, 1)
    own, own_live = [], []
    for i in range(NCOL):
        pick = jnp.where(iota((128, COLS), 1) == first_col + i, 1.0, 0.0).astype(BF16)
        hit = jnp.where(dot(pick, ids, 1, 1) == token, 1.0, 0.0)
        own.append(hit.astype(BF16))
        own_live.append((hit * live_row).astype(BF16))
    wm_s[640:768, :] = jnp.concatenate(own, axis=1)
    picked = dot(sc_s[...], jnp.concatenate(own_live, axis=1)).astype(BF16)
    sums = [None] * 4
    for b in range(VOCAB):
        left = jnp.concatenate([
            picked[at + b * HP:at + (b + 1) * HP, i * ROWS:(i + 1) * ROWS]
            for at in (0, VH) for i in range(NCOL)], axis=0)
        term = dot(left, onehot(ids, b))
        sums[b % 4] = term if sums[b % 4] is None else sums[b % 4] + term
    tied4 = (sums[0] + sums[1]) + (sums[2] + sums[3])
    tied = tied4[0:NCOL * HP] + tied4[NCOL * HP:]
    tied = tied * (HEAD_DIM ** (-0.5) * lax.rsqrt(count))
    top = jnp.max(tied, axis=1, keepdims=True)
    weights = jnp.exp(tied - top)
    scale = 1.0 / jnp.sum(weights, axis=1, keepdims=True)
    weights = weights.astype(BF16)

    for b in range(VOCAB):
        share = dot(weights, onehot(ids_t, b)) * scale
        for i in range(NCOL):
            wm_s[b * HP:(b + 1) * HP, i * ROWS:(i + 1) * ROWS] = share[i * HP:(i + 1) * HP].astype(BF16)

    fetch[5].wait()
    row_share.receive()
    col_weight = cqkv_ref[...].reshape(3 * DH, D)
    live_here = live2 > 0.0

    mixed = dot(vo_s[...].reshape(D, D), wm_s[...])
    near = [mixed[:, i * ROWS:i * ROWS + 128] for i in range(NCOL)]
    for q in range(NX):
        pair = near[q // 2 * 2:q // 2 * 2 + 2]
        at = slice(q % 2 * 64, q % 2 * 64 + 64)
        mixed_s[q] = jnp.concatenate([pair[0][:, at], pair[1][:, at]], axis=1)
    normed2 = norm_cols(mixed).astype(BF16)
    proj = dot(col_weight[DH:], normed2)
    query = dot(col_weight[:DH], jnp.concatenate(
        [normed2[:, i * ROWS:i * ROWS + 128] for i in range(NCOL)], axis=1))
    query = query.astype(BF16) * jnp.asarray(0.125, BF16)
    keys, queries, values = [], [], []
    for i in range(NCOL):
        at = slice(i * ROWS, (i + 1) * ROWS)
        key = proj[0:DH, at].astype(BF16)
        value = proj[DH:2 * DH, at].astype(BF16)
        for h in range(0, DH, HEAD_DIM):
            keys.append(key[h:h + HEAD_DIM])
            values.append(value[h:h + HEAD_DIM])
            queries.append(query[h:h + HEAD_DIM, i * 128:i * 128 + 128])
    blank = jnp.zeros((HEAD_DIM, 128), BF16)
    scores = []
    for q in range(0, 3 * NCOL, 2):
        both = jnp.concatenate([
            jnp.concatenate([queries[q], blank], axis=1), jnp.concatenate([blank, queries[q + 1]], axis=1)], axis=0)
        scores.append(dot(jnp.concatenate(keys[q:q + 2], axis=0), both, 0, 0))
    got = []
    weighted, totals = [], []
    for score in scores:
        score = jnp.where(live_here, score, -1e38)
        raw = jnp.exp(score - jnp.max(score, axis=0, keepdims=True))
        totals.append(1.0 / jnp.sum(raw, axis=0, keepdims=True))
        weighted.append(raw.astype(BF16))
    for q in range(0, 3 * NCOL, 2):
        both = dot(jnp.concatenate(values[q:q + 2], axis=0), weighted[q // 2]) * totals[q // 2]
        got += [both[0:HEAD_DIM, 0:128], both[HEAD_DIM:, 128:256]]
    for q in range(NX):
        for h in range(3):
            pair = [got[(q // 2 * 2 + c) * 3 + h][:, q % 2 * 64:q % 2 * 64 + 64] for c in range(2)]
            ctxs[q, h * HEAD_DIM:(h + 1) * HEAD_DIM, :] = jnp.concatenate(pair, axis=1).astype(BF16)
    to_slot = Exchange(
        lambda k: remote(ctxs.at[ahead(k)], ctxr.at[x], xs.at[k], xr.at[k], s, ahead(k)),
        lambda k: remote(ctxs.at[ahead(k)], ctxr.at[behind(k)], xs.at[k], xr.at[k], s, ahead(k)),
        FAR_X)
    to_slot.start()
    col_share = forward(wco, cfs, cfr)
    col_out.receive()
    col_share.start()
    ctxr[x] = ctxs[x]

    fetch[6].wait()
    col_share.receive()
    to_slot.receive()

    context = ctxr[...].reshape(D, 128)

    def a_place(j):
        to_x = lax.rem(x + j // 4, NX)
        to_half = lax.rem(y + (j // 2) % 2, 2)
        return to_x, to_half, lax.rem(core + j % 2, 2)

    def a_out(j):
        to_x, to_half, to_core = a_place(j)
        k = grp * 2 + col_in
        return remote(
            sa.at[j // 4, to_half * 2 + to_core], ra.at[k], as_.at[j], ar.at[k],
            seq_at(2 * half + to_half, z, to_core), to_x)

    def a_into(j):
        from_y = lax.rem(y + j // 4, NY)
        from_core = lax.rem(core + j % 2, 2)
        from_col = lax.rem(col_in + (j // 2) % 2, 2)
        k = (from_y * NC + from_core) * 2 + from_col
        return remote(
            ra.at[k], ra.at[k], as_.at[j], ar.at[k], seq_at(from_y, z, from_core), 2 * from_col + lax.div(y, 2))

    stays = half == lax.div(y, 2)
    to_plane = Exchange(
        a_out, a_into, FAR_PLANE,
        lambda j: jnp.logical_not(stays) if j == 0 else None,
        lambda j: jnp.logical_not(stays) if j == 0 else None)
    for step in (2, 1, 3, 0):
        to_x = lax.rem(x + step, NX)
        rows = pl.ds(pl.multiple_of(to_x * DH, DH), DH)
        turned = (dot(wco[to_x], context) + mixed_s[x, rows, :]).T
        for g in range(4):
            rows_of = [jnp.concatenate([turned[r + g * 8:r + g * 8 + 8], turned[64 + r + g * 8:64 + r + g * 8 + 8]], axis=0)
                       for r in (0, 32)]
            sa[step, g] = jnp.concatenate(rows_of, axis=1).astype(BF16)
        to_plane.start([j for j in FAR_PLANE if j // 4 == step])

    @pl.when(stays)
    def _():
        ra[grp * 2 + col_in] = sa[0, lax.rem(y, 2) * 2 + core]

    order = iota((256, 256), 0)
    swap = jnp.where(lax.rem(order, 32) * 8 + lax.div(order, 32) == iota((256, 256), 1), 1.0, 0.0).astype(BF16)
    to_plane.receive()

    sb[...] = dot(swap, ra[...].reshape(256, 384)).astype(BF16)

    def near_part(step):
        return pl.ds(pl.multiple_of((step + 4 - odd) * 32, 32), 32)

    def col_part(at):
        return pl.ds(pl.multiple_of(lax.rem(at, 8) * 32, 32), 32)

    side = 1 - 2 * odd
    to_rows = Exchange(
        lambda k: remote(
            sb.at[near_part(side * k), :], out_ref.at[col_part(z), :], bs.at[k + 4], br.at[side * k + 4],
            seq_at(y, lax.rem(z + NZ + side * k, NZ), core), x),
        lambda k: remote(
            sb.at[near_part(side * k), :], out_ref.at[col_part(z + NZ - side * k), :], bs.at[k + 4], br.at[side * k + 4],
            seq_at(y, lax.rem(z + NZ + side * k, NZ), core), x),
        NEAR_Z)
    to_rows.start()
    keep = pltpu.make_async_copy(sb.at[near_part(0), :], out_ref.at[col_part(z), :], ls.at[7])
    keep.start()

    ids_z.finish()
    ids_up.finish()
    ids_down.finish()
    ids_y.finish()
    tabs.finish()
    for weights_sent in (row_out, col_out, row_share, col_share):
        weights_sent.finish()
    to_slot.finish()
    to_plane.finish()
    keep.wait()
    to_rows.finish()
    to_rows.receive()


def body(ids, pad_mask, embed, row_qkv, row_out, col_qkv, col_out):
    dma = pltpu.SemaphoreType.DMA
    got = pl.pallas_call(
        kernel,
        out_shape=pltpu.VMEM((COLS, 2 * DH), BF16),
        in_specs=[pl.BlockSpec(memory_space=pltpu.HBM)] * 7,
        out_specs=pl.BlockSpec(memory_space=pl.ANY),
        scratch_shapes=[
            pltpu.VMEM((2, COLS), jnp.int32),
            pltpu.SMEM((2,), jnp.int32),
            pltpu.VMEM((VOCAB, D), BF16),
            pltpu.VMEM((3, DH, D), BF16),
            pltpu.VMEM((3, DH, D), BF16),
            pltpu.VMEM((128, 1, 384), jnp.int32),
            pltpu.VMEM((NX, 144, 256), BF16),
            pltpu.VMEM((NX, DH, D), BF16),
            pltpu.VMEM((NX, DH, D), BF16),
            pltpu.VMEM((128, D), F32),
            pltpu.VMEM((1024, D), BF16),
            pltpu.VMEM((128, D), BF16),
            pltpu.VMEM((48, D), F32),
            pltpu.VMEM((128, D), F32),
            pltpu.VMEM((VH, D), BF16),
            pltpu.VMEM((D, 640), BF16),
            pltpu.VMEM((D, NCOL * ROWS), BF16),
            pltpu.VMEM((NX, DH, D), BF16),
            pltpu.VMEM((2 * VH, 128), BF16),
            pltpu.VMEM((4, D, 128), F32),
            pltpu.VMEM((NX, DH, 128), BF16),
            pltpu.VMEM((NX, DH, 128), BF16),
            pltpu.VMEM((NX, 4, 16, 384), BF16),
            pltpu.VMEM((16, 16, 384), BF16),
            pltpu.VMEM((256, 384), BF16),
            dma((16,)), dma((16,)),
            dma((8,)), dma((8,)),
            dma((4,)), dma((4,)),
            dma((4,)), dma((4,)), dma((4,)), dma((4,)),
            dma((4,)), dma((4,)), dma((4,)), dma((4,)),
            dma((4,)), dma((4,)),
            dma((16,)), dma((16,)),
            dma((16,)), dma((16,)),
            dma((8,)),
        ],
        compiler_params=pltpu.CompilerParams(
            collective_id=0, has_side_effects=True, vmem_limit_bytes=63 * 1024 * 1024),
        cost_estimate=pl.CostEstimate(flops=6_000_000_000, bytes_accessed=4_000_000, transcendentals=500_000),
        name="msa_layer",
    )(ids, pad_mask, embed, row_qkv, row_out, col_qkv, col_out)
    return jnp.transpose(got.reshape(COLS, 2, DH), (1, 0, 2))


def solution(mesh):
    placed = (
        P("seq", None),
        P("seq"),
        P(),
        P(None, "head", None),
        P("head", None),
        P(None, "head", None),
        P("head", None),
    )
    return jax.shard_map(
        body, mesh=mesh, in_specs=placed, out_specs=P("seq", None, "head"), check_vma=False
    )
```

```python
import jax
import jax.numpy as jnp
from jax import lax
from jax.experimental import pallas as pl
from jax.experimental.pallas import tpu as pltpu
from jax.sharding import PartitionSpec as P

HEAD_DIM = 64
EPS = 1e-05
NX, NY, NZ, NC = 4, 4, 16, 2
VOCAB = 33
D = 768
DH = 192
COLS = 256
ROWS = 256
HP = 16
VH = VOCAB * HP
DIRECT_Z = (4, -4, 3, -3, 2, -2, 1, -1)
FAR_Y = (4, 5, 3, 2, 6, 7, 1)
NEAR_Z = (-4, 3, -3, 2, -2, 1, -1)
NCOL = 4
FAR_X = (2, 1, 3)
FAR_PLANE = (10, 11, 8, 9, 6, 7, 14, 15, 4, 5, 12, 13, 2, 3, 1, 0)
MESH = pl.DeviceIdType.MESH
F32 = jnp.float32
BF16 = jnp.bfloat16


def dot(a, b, ca=1, cb=0):
    return lax.dot_general(a, b, (((ca,), (cb,)), ((), ())), preferred_element_type=F32)


def norm_rows(values):
    mean = jnp.mean(values, axis=1, keepdims=True)
    centred = values - mean
    spread = jnp.mean(centred * centred, axis=1, keepdims=True)
    return centred * lax.rsqrt(spread + EPS)


def norm_cols(values):
    mean = jnp.mean(values, axis=0, keepdims=True)
    centred = values - mean
    spread = jnp.mean(centred * centred, axis=0, keepdims=True)
    return centred * lax.rsqrt(spread + EPS)


def iota(shape, dim):
    return lax.broadcasted_iota(jnp.int32, shape, dim)


class Exchange:
    opened = []

    def __init__(self, out, into, keys, sends=None, arrives=None):
        self.out, self.into, self.keys = out, into, keys
        self.sends = sends or (lambda k: None)
        self.arrives = arrives or (lambda k: None)
        Exchange.opened.append(self)
        self.waited = False

    def each(self, run, keys=None):
        for k in self.keys if keys is None else keys:
            run(k)

    def start(self, keys=None):
        def run(k):
            gate(self.sends(k), lambda: self.out(k).start())
        self.each(run, keys)

    def receive(self, keys=None):
        self.waited = True

        def run(k):
            gate(self.arrives(k), lambda: self.into(k).wait_recv())
        self.each(run, self.keys[::-1] if keys is None else keys)

    def finish(self):
        def run(k):
            gate(self.sends(k), lambda: self.out(k).wait_send())
        self.each(run)


def gate(condition, action):
    if condition is None:
        action()
    else:
        pl.when(condition)(action)


def kernel(
    ids_hbm, mask_hbm, embed_hbm, rqkv_hbm, rout_hbm, cqkv_hbm, cout_hbm,
    out_ref,
    ids_ref, mask_ref, embed_ref, rqkv_ref, cqkv_ref,
    idbuf, tab, wro, wco, emb_s, sel_s, qt_s, kf_s, vf_s, kx_s, vxt_s, wm_s, vo_s, sc_s,
    mixed_s, ctxs, ctxr, sa, ra, sb,
    zs, zr, ys, yr, ts, tr, ros, ror, rfs, rfr, cos, cor, cfs, cfr, xs, xr, as_, ar, bs, br, ls,
):
    Exchange.opened = []
    s = lax.axis_index("seq")
    x = lax.axis_index("head")
    y = lax.div(s, NZ * NC)
    z = lax.rem(lax.div(s, NC), NZ)
    core = lax.rem(s, NC)
    grp = y * NC + core
    half = lax.rem(x, 2)
    col_in = lax.div(x, 2)
    odd = lax.rem(z, 2)
    first_z = lax.rem(z + NZ - 4 + odd, NZ)

    def seq_at(yy, zz, cc):
        return (yy * NZ + zz) * NC + cc

    def remote(src, dst, ss, rs, to_s, to_x):
        return pltpu.make_async_remote_copy(
            src_ref=src, dst_ref=dst, send_sem=ss, recv_sem=rs, device_id=(to_s, to_x), device_id_type=MESH)

    fetch = [
        pltpu.make_async_copy(a, b, ls.at[i]) for i, (a, b) in enumerate((
            (ids_hbm, ids_ref), (mask_hbm, mask_ref), (embed_hbm, embed_ref), (rqkv_hbm, rqkv_ref),
            (rout_hbm, wro.at[x]), (cqkv_hbm, cqkv_ref), (cout_hbm, wco.at[x])))
    ]
    fetch[0].start()
    fetch[1].start()
    barrier = pltpu.get_barrier_semaphore()

    for k in DIRECT_Z:
        pl.semaphore_signal(
            barrier, inc=1, device_id=(seq_at(y, lax.rem(z + NZ + k, NZ), core), x), device_id_type=MESH)

    def greet_plane(k, carry):
        place = lax.rem(x * 8 + grp + k, 32)
        px, pg = lax.div(place, 8), lax.rem(place, 8)
        pl.semaphore_signal(
            barrier, inc=1, device_id=(seq_at(lax.div(pg, NC), z, lax.rem(pg, NC)), px), device_id_type=MESH)
        return carry

    lax.fori_loop(1, 32, greet_plane, 0)
    for copy in fetch[2:]:
        copy.start()

    slot = grp * NZ + z
    fetch[0].wait()
    fetch[1].wait()
    m0 = mask_ref[0]
    m1 = mask_ref[1]
    idbuf[slot, :, 0:COLS] = ids_ref[0:1, :] + ids_ref[1:2, :] * 65536
    idbuf[slot, :, COLS:COLS + 128] = jnp.zeros((1, 128), jnp.int32) + (m0 + m1 * 65536)

    pl.semaphore_wait(barrier, len(DIRECT_Z) + 31)

    def z_slot(k):
        return idbuf.at[grp * NZ + lax.rem(z + NZ + k, NZ)]

    def z_seq(k):
        return seq_at(y, lax.rem(z + NZ + k, NZ), core)

    ids_z = Exchange(
        lambda k: remote(z_slot(0), z_slot(0), zs.at[k + 4], zr.at[k + 4], z_seq(k), x),
        lambda k: remote(z_slot(-k), z_slot(-k), zs.at[k + 4], zr.at[k + 4], z_seq(k), x),
        DIRECT_Z)
    ids_down = Exchange(
        lambda k: remote(z_slot(k), z_slot(k), zs.at[8 + k], zr.at[8 + k], z_seq(-4), x),
        lambda k: remote(z_slot(4 + k), z_slot(4 + k), zs.at[8 + k], zr.at[8 + k], z_seq(-4), x),
        (4, 3, 2, 1))
    ids_up = Exchange(
        lambda k: remote(z_slot(-k), z_slot(-k), zs.at[12 + k], zr.at[12 + k], z_seq(4), x),
        lambda k: remote(z_slot(-4 - k), z_slot(-4 - k), zs.at[12 + k], zr.at[12 + k], z_seq(4), x),
        (3, 2, 1))
    ids_z.start()

    fetch[2].wait()
    emb_s[...] = jnp.zeros_like(emb_s)
    emb_s[0:VOCAB, :] = embed_ref[...].astype(F32)
    normed = norm_rows(emb_s[...]).astype(BF16)[0:48, :]
    tab[x] = jnp.zeros((112, 256), BF16)
    fetch[3].wait()
    tab[x, :, 0:DH] = jnp.concatenate(
        [dot(normed, rqkv_ref[t], 1, 1)[0:VOCAB] for t in range(3)] + [jnp.zeros((112 - 3 * VOCAB, DH), F32)],
        axis=0).astype(BF16)

    part = pl.ds(pl.multiple_of(core * 96, 96), 96)
    other = pl.ds(pl.multiple_of((1 - core) * 96, 96), 96)
    ahead = lambda k: lax.rem(x + k, NX)
    behind = lambda k: lax.rem(x + NX - k, NX)

    def weight(src, buf, ss, rs):
        return Exchange(
            lambda k: remote(src.at[part, :], buf.at[x, part, :], ss.at[k], rs.at[k], s, ahead(k)),
            lambda k: remote(src.at[part, :], buf.at[behind(k), part, :], ss.at[k], rs.at[k], s, ahead(k)),
            FAR_X)

    def forward(buf, ss, rs):
        twin = s + 1 - 2 * core
        return Exchange(
            lambda k: remote(
                buf.at[behind(k), part, :], buf.at[behind(k), part, :], ss.at[k], rs.at[k], twin, x),
            lambda k: remote(
                buf.at[behind(k), other, :], buf.at[behind(k), other, :], ss.at[k], rs.at[k], twin, x),
            FAR_X)

    tabs = Exchange(
        lambda k: remote(tab.at[x], tab.at[x], ts.at[k], tr.at[k], s, ahead(k)),
        lambda k: remote(tab.at[behind(k)], tab.at[behind(k)], ts.at[k], tr.at[k], s, ahead(k)),
        FAR_X)
    tabs.start()
    row_out = weight(rout_hbm, wro, ros, ror)
    row_out.start()
    col_out = weight(cout_hbm, wco, cos, cor)

    vo_s[:, :, 640:768] = emb_s[...].T.astype(BF16).reshape(NX, DH, 128)
    spot = iota((4 * 256, D), 0)
    goal = lax.div(spot, 256) * DH + lax.rem(spot, 256)
    sel_s[...] = jnp.where(
        jnp.logical_and(goal == iota((4 * 256, D), 1), lax.rem(spot, 256) < DH), 1.0, 0.0).astype(BF16)

    ids_z.receive((1, 2, 3))
    ids_up.start()
    ids_z.receive((-1, -2, -3, -4))
    ids_down.start()
    ids_z.receive((4,))
    ids_up.receive()
    ids_down.receive()
    mine = pl.ds(grp * NZ, NZ)

    def y_seq(k):
        to = lax.rem(grp + k, 8)
        return seq_at(lax.div(to, NC), z, lax.rem(to, NC))

    def y_part(k):
        return idbuf.at[pl.ds(lax.rem(grp + 8 - k, 8) * NZ, NZ)]

    ids_y = Exchange(
        lambda k: remote(idbuf.at[mine], idbuf.at[mine], ys.at[k], yr.at[k], y_seq(k), x),
        lambda k: remote(y_part(k), y_part(k), ys.at[k], yr.at[k], y_seq(k), x),
        FAR_Y)
    ids_y.start()
    col_out.start()

    tabs.receive()
    gathered = jnp.concatenate([tab[i] for i in range(NX)], axis=1)
    tables = dot(gathered, sel_s[...])
    qt_s[...] = jnp.zeros_like(qt_s)
    qt_s[0:48, :] = jnp.concatenate([tables[0:VOCAB], jnp.zeros((48 - VOCAB, D), F32)], axis=0).astype(BF16)
    kf_s[0:VOCAB, :] = tables[VOCAB:2 * VOCAB]
    vf_s[...] = jnp.zeros_like(vf_s)
    vf_s[0:VOCAB, :] = tables[2 * VOCAB:3 * VOCAB]
    own_head = jnp.where(iota((HP, D), 0) == lax.div(iota((HP, D), 1), HEAD_DIM), 1.0, 0.0)

    def expand(b, carry):
        kx_s[pl.ds(pl.multiple_of(b * HP, HP), HP), :] = (kf_s[pl.ds(b, 1), :] * own_head).astype(BF16)
        return carry

    lax.fori_loop(0, VOCAB, expand, 0)
    scores_of = dot(kx_s[...], qt_s[...], 1, 1)
    upper = scores_of.astype(BF16)
    sc_s[0:VH, :] = upper
    sc_s[VH:2 * VH, :] = (scores_of - upper.astype(F32)).astype(BF16)
    rep = jnp.where(iota((128, 640), 0) == lax.div(iota((128, 640), 1), HP), 1.0, 0.0).astype(BF16)
    head_of = jnp.where(
        lax.div(iota((D, 640), 0), HEAD_DIM) == lax.rem(iota((D, 640), 1), HP), 1.0, 0.0)
    vxt_s[...] = (dot(vf_s[...].T.astype(BF16), rep) * head_of).astype(BF16)
    wm_s[VH:640, :] = jnp.zeros((640 - VH, NCOL * ROWS), BF16)

    row_out.receive()
    fetch[4].wait()
    vo_s[:, part, 0:640] = dot(wro[:, part, :].reshape(4 * 96, D), vxt_s[...]).astype(BF16).reshape(4, 96, 640)
    twin = s + 1 - 2 * core
    row_share = Exchange(
        lambda k: remote(
            vo_s.at[:, part, pl.ds(0, 640)], vo_s.at[:, part, pl.ds(0, 640)], rfs.at[k], rfr.at[k], twin, x),
        lambda k: remote(
            vo_s.at[:, other, pl.ds(0, 640)], vo_s.at[:, other, pl.ds(0, 640)], rfs.at[k], rfr.at[k], twin, x),
        (0,))
    row_share.start()

    ids_y.receive()

    words = idbuf[:, 0, :]
    low = lax.bitwise_and(words, 65535).astype(F32)
    high = lax.shift_right_logical(words, 16).astype(F32)
    table = jnp.concatenate([low[0:64], high[0:64], low[64:128], high[64:128]], axis=0)
    place = iota((ROWS, ROWS), 0)
    from_z = lax.rem(lax.div(place, 128) * 8 + lax.rem(place, 8) + first_z, NZ)
    from_row = lax.rem(lax.div(place, 64), 2) * 128 + lax.rem(lax.div(place, 8), 8) * 16 + from_z
    shuffle = jnp.where(from_row == iota((ROWS, ROWS), 1), 1.0, 0.0).astype(BF16)
    table = dot(shuffle, table.astype(BF16))
    ids = table[:, 0:COLS].astype(BF16)
    live = table[:, COLS:COLS + 128]
    live2 = jnp.concatenate([live, live], axis=1)
    eye = jnp.where(iota((COLS, COLS), 0) == iota((COLS, COLS), 1), 1.0, 0.0).astype(BF16)
    ids_t = dot(eye, ids, 1, 1).astype(BF16)

    def onehot(of, b):
        return jnp.where(of == jnp.asarray(b, BF16), jnp.asarray(1, BF16), jnp.asarray(0, BF16))

    count = jnp.sum(live2, axis=0, keepdims=True)
    first_col = lax.rem(z, 8) * 32 + grp * NCOL
    token = iota((128, ROWS), 0).astype(F32)
    first_lane = jnp.where(iota((128, 128), 1) == 0, 1.0, 0.0).astype(BF16)
    live_row = dot(first_lane, live.astype(BF16), 1, 1)
    own, own_live = [], []
    for i in range(NCOL):
        pick = jnp.where(iota((128, COLS), 1) == first_col + i, 1.0, 0.0).astype(BF16)
        hit = jnp.where(dot(pick, ids, 1, 1) == token, 1.0, 0.0)
        own.append(hit.astype(BF16))
        own_live.append((hit * live_row).astype(BF16))
    wm_s[640:768, :] = jnp.concatenate(own, axis=1)
    picked = dot(sc_s[...], jnp.concatenate(own_live, axis=1)).astype(BF16)
    sums = [None] * 4
    for b in range(VOCAB):
        left = jnp.concatenate([
            picked[at + b * HP:at + (b + 1) * HP, i * ROWS:(i + 1) * ROWS]
            for at in (0, VH) for i in range(NCOL)], axis=0)
        term = dot(left, onehot(ids, b))
        sums[b % 4] = term if sums[b % 4] is None else sums[b % 4] + term
    tied4 = (sums[0] + sums[1]) + (sums[2] + sums[3])
    tied = tied4[0:NCOL * HP] + tied4[NCOL * HP:]
    tied = tied * (HEAD_DIM ** (-0.5) * lax.rsqrt(count))
    top = jnp.max(tied, axis=1, keepdims=True)
    weights = jnp.exp(tied - top)
    scale = 1.0 / jnp.sum(weights, axis=1, keepdims=True)
    weights = weights.astype(BF16)

    for b in range(VOCAB):
        share = dot(weights, onehot(ids_t, b)) * scale
        for i in range(NCOL):
            wm_s[b * HP:(b + 1) * HP, i * ROWS:(i + 1) * ROWS] = share[i * HP:(i + 1) * HP].astype(BF16)

    fetch[5].wait()
    row_share.receive()
    col_weight = cqkv_ref[...].reshape(3 * DH, D)
    live_here = live2 > 0.0

    mixed = dot(vo_s[...].reshape(D, D), wm_s[...])
    near = [mixed[:, i * ROWS:i * ROWS + 128] for i in range(NCOL)]
    for q in range(NX):
        pair = near[q // 2 * 2:q // 2 * 2 + 2]
        at = slice(q % 2 * 64, q % 2 * 64 + 64)
        mixed_s[q] = jnp.concatenate([pair[0][:, at], pair[1][:, at]], axis=1)
    normed2 = norm_cols(mixed).astype(BF16)
    proj = dot(col_weight[DH:], normed2)
    query = dot(col_weight[:DH], jnp.concatenate(
        [normed2[:, i * ROWS:i * ROWS + 128] for i in range(NCOL)], axis=1))
    query = query.astype(BF16) * jnp.asarray(0.125, BF16)
    keys, queries, values = [], [], []
    for i in range(NCOL):
        at = slice(i * ROWS, (i + 1) * ROWS)
        key = proj[0:DH, at].astype(BF16)
        value = proj[DH:2 * DH, at].astype(BF16)
        for h in range(0, DH, HEAD_DIM):
            keys.append(key[h:h + HEAD_DIM])
            values.append(value[h:h + HEAD_DIM])
            queries.append(query[h:h + HEAD_DIM, i * 128:i * 128 + 128])
    blank = jnp.zeros((HEAD_DIM, 128), BF16)
    scores = []
    for q in range(0, 3 * NCOL, 2):
        both = jnp.concatenate([
            jnp.concatenate([queries[q], blank], axis=1), jnp.concatenate([blank, queries[q + 1]], axis=1)], axis=0)
        scores.append(dot(jnp.concatenate(keys[q:q + 2], axis=0), both, 0, 0))
    got = []
    weighted, totals = [], []
    for score in scores:
        score = jnp.where(live_here, score, -1e38)
        raw = jnp.exp(score - jnp.max(score, axis=0, keepdims=True))
        totals.append(1.0 / jnp.sum(raw, axis=0, keepdims=True))
        weighted.append(raw.astype(BF16))
    for q in range(0, 3 * NCOL, 2):
        both = dot(jnp.concatenate(values[q:q + 2], axis=0), weighted[q // 2]) * totals[q // 2]
        got += [both[0:HEAD_DIM, 0:128], both[HEAD_DIM:, 128:256]]
    for q in range(NX):
        for h in range(3):
            pair = [got[(q // 2 * 2 + c) * 3 + h][:, q % 2 * 64:q % 2 * 64 + 64] for c in range(2)]
            ctxs[q, h * HEAD_DIM:(h + 1) * HEAD_DIM, :] = jnp.concatenate(pair, axis=1).astype(BF16)
    to_slot = Exchange(
        lambda k: remote(ctxs.at[ahead(k)], ctxr.at[x], xs.at[k], xr.at[k], s, ahead(k)),
        lambda k: remote(ctxs.at[ahead(k)], ctxr.at[behind(k)], xs.at[k], xr.at[k], s, ahead(k)),
        FAR_X)
    to_slot.start()
    col_share = forward(wco, cfs, cfr)
    col_out.receive()
    col_share.start()
    ctxr[x] = ctxs[x]

    fetch[6].wait()
    col_share.receive()
    to_slot.receive()

    context = ctxr[...].reshape(D, 128)

    def a_place(j):
        to_x = lax.rem(x + j // 4, NX)
        to_half = lax.rem(y + (j // 2) % 2, 2)
        return to_x, to_half, lax.rem(core + j % 2, 2)

    def a_out(j):
        to_x, to_half, to_core = a_place(j)
        k = grp * 2 + col_in
        return remote(
            sa.at[j // 4, to_half * 2 + to_core], ra.at[k], as_.at[j], ar.at[k],
            seq_at(2 * half + to_half, z, to_core), to_x)

    def a_into(j):
        from_y = lax.rem(y + j // 4, NY)
        from_core = lax.rem(core + j % 2, 2)
        from_col = lax.rem(col_in + (j // 2) % 2, 2)
        k = (from_y * NC + from_core) * 2 + from_col
        return remote(
            ra.at[k], ra.at[k], as_.at[j], ar.at[k], seq_at(from_y, z, from_core), 2 * from_col + lax.div(y, 2))

    stays = half == lax.div(y, 2)
    to_plane = Exchange(
        a_out, a_into, FAR_PLANE,
        lambda j: jnp.logical_not(stays) if j == 0 else None,
        lambda j: jnp.logical_not(stays) if j == 0 else None)
    for step in (2, 1, 3, 0):
        to_x = lax.rem(x + step, NX)
        rows = pl.ds(pl.multiple_of(to_x * DH, DH), DH)
        turned = (dot(wco[to_x], context) + mixed_s[x, rows, :]).T
        for g in range(4):
            rows_of = [jnp.concatenate([turned[r + g * 8:r + g * 8 + 8], turned[64 + r + g * 8:64 + r + g * 8 + 8]], axis=0)
                       for r in (0, 32)]
            sa[step, g] = jnp.concatenate(rows_of, axis=1).astype(BF16)
        to_plane.start([j for j in FAR_PLANE if j // 4 == step])

    @pl.when(stays)
    def _():
        ra[grp * 2 + col_in] = sa[0, lax.rem(y, 2) * 2 + core]

    order = iota((256, 256), 0)
    swap = jnp.where(lax.rem(order, 32) * 8 + lax.div(order, 32) == iota((256, 256), 1), 1.0, 0.0).astype(BF16)
    to_plane.receive()

    sb[...] = dot(swap, ra[...].reshape(256, 384)).astype(BF16)

    def near_part(step):
        return pl.ds(pl.multiple_of((step + 4 - odd) * 32, 32), 32)

    def col_part(at):
        return pl.ds(pl.multiple_of(lax.rem(at, 8) * 32, 32), 32)

    side = 1 - 2 * odd
    to_rows = Exchange(
        lambda k: remote(
            sb.at[near_part(side * k), :], out_ref.at[col_part(z), :], bs.at[k + 4], br.at[side * k + 4],
            seq_at(y, lax.rem(z + NZ + side * k, NZ), core), x),
        lambda k: remote(
            sb.at[near_part(side * k), :], out_ref.at[col_part(z + NZ - side * k), :], bs.at[k + 4], br.at[side * k + 4],
            seq_at(y, lax.rem(z + NZ + side * k, NZ), core), x),
        NEAR_Z)
    to_rows.start()
    keep = pltpu.make_async_copy(sb.at[near_part(0), :], out_ref.at[col_part(z), :], ls.at[7])
    keep.start()

    ids_z.finish()
    ids_up.finish()
    ids_down.finish()
    ids_y.finish()
    tabs.finish()
    for weights_sent in (row_out, col_out, row_share, col_share):
        weights_sent.finish()
    to_slot.finish()
    to_plane.finish()
    keep.wait()
    to_rows.finish()
    to_rows.receive()


def body(ids, pad_mask, embed, row_qkv, row_out, col_qkv, col_out):
    dma = pltpu.SemaphoreType.DMA
    got = pl.pallas_call(
        kernel,
        out_shape=pltpu.VMEM((COLS, 2 * DH), BF16),
        in_specs=[pl.BlockSpec(memory_space=pltpu.HBM)] * 7,
        out_specs=pl.BlockSpec(memory_space=pl.ANY),
        scratch_shapes=[
            pltpu.VMEM((2, COLS), jnp.int32),
            pltpu.SMEM((2,), jnp.int32),
            pltpu.VMEM((VOCAB, D), BF16),
            pltpu.VMEM((3, DH, D), BF16),
            pltpu.VMEM((3, DH, D), BF16),
            pltpu.VMEM((128, 1, 384), jnp.int32),
            pltpu.VMEM((NX, 112, 256), BF16),
            pltpu.VMEM((NX, DH, D), BF16),
            pltpu.VMEM((NX, DH, D), BF16),
            pltpu.VMEM((128, D), F32),
            pltpu.VMEM((1024, D), BF16),
            pltpu.VMEM((128, D), BF16),
            pltpu.VMEM((48, D), F32),
            pltpu.VMEM((128, D), F32),
            pltpu.VMEM((VH, D), BF16),
            pltpu.VMEM((D, 640), BF16),
            pltpu.VMEM((D, NCOL * ROWS), BF16),
            pltpu.VMEM((NX, DH, D), BF16),
            pltpu.VMEM((2 * VH, 128), BF16),
            pltpu.VMEM((4, D, 128), F32),
            pltpu.VMEM((NX, DH, 128), BF16),
            pltpu.VMEM((NX, DH, 128), BF16),
            pltpu.VMEM((NX, 4, 16, 384), BF16),
            pltpu.VMEM((16, 16, 384), BF16),
            pltpu.VMEM((256, 384), BF16),
            dma((16,)), dma((16,)),
            dma((8,)), dma((8,)),
            dma((4,)), dma((4,)),
            dma((4,)), dma((4,)), dma((4,)), dma((4,)),
            dma((4,)), dma((4,)), dma((4,)), dma((4,)),
            dma((4,)), dma((4,)),
            dma((16,)), dma((16,)),
            dma((16,)), dma((16,)),
            dma((8,)),
        ],
        compiler_params=pltpu.CompilerParams(
            collective_id=0, has_side_effects=True, vmem_limit_bytes=63 * 1024 * 1024),
        cost_estimate=pl.CostEstimate(flops=6_000_000_000, bytes_accessed=4_000_000, transcendentals=500_000),
        name="msa_layer",
    )(ids, pad_mask, embed, row_qkv, row_out, col_qkv, col_out)
    return jnp.transpose(got.reshape(COLS, 2, DH), (1, 0, 2))


def solution(mesh):
    placed = (
        P("seq", None),
        P("seq"),
        P(),
        P(None, "head", None),
        P("head", None),
        P(None, "head", None),
        P("head", None),
    )
    return jax.shard_map(
        body, mesh=mesh, in_specs=placed, out_specs=P("seq", None, "head"), check_vma=False
    )
```
